256 devices in a mesh: row: 8 (over z), col: 16 (over x, y), rep: 2 (over core).
Axes of the slice: x: 4, y: 4, z: 8, core: 2. Of those that a mesh axis runs over, the one named last changes fastest.
Arguments:
- density: bfloat16 [6144, 6144], P('row', 'col')
- pattern: int32 [48, 48], replicated, may hold values from 0 to 1, as said below
- keep: int32 [2, 48, 48], replicated, may hold values from 0 to 1, as said below
Outputs:
- purified: bfloat16 [6144, 6144], P('row', 'col')
The draws below stay inside these ranges and needn't reach their ends.
Inputs may be any that keep to these rules, and one draw needn't show every extreme that they name: density is symmetric. pattern is symmetric, 0 or 1, with ones on the diagonal. Each keep[s] is symmetric, 0 or 1, with ones on the diagonal.
All inputs are finite; a program needn't handle non-finite values.
Results may differ from the reference program's by a relative error of at most 0.0057.
Values may be sent and summed in bfloat16 or wider, within the bound.
A program may use at most 64 MiB of HBM per device.

```python
import jax
import jax.numpy as jnp

BS = 128
NB = 48


def symmetric_mask(key, ones_of_four, heavy):
    index = jnp.arange(NB)
    upper = jax.random.randint(key, (NB, NB), 0, 4)
    near = jnp.abs(index[:, None] - index[None, :]) <= max(NB // 8, 1)
    rich = (index[:, None] < heavy) | (index[None, :] < heavy)
    limit = jnp.where(rich, 3, ones_of_four)
    chosen = jnp.where(near | (upper < limit), 1, 0).astype(jnp.int32)
    upper_part = jnp.triu(chosen)
    return jnp.maximum(upper_part, upper_part.T)


def draw_pattern(key, part):
    key = jax.random.fold_in(key, 1)
    return symmetric_mask(key, 1, max(NB // 4, 1))


def draw_keep(key, part):
    key = jax.random.fold_in(key, 2)
    first = symmetric_mask(jax.random.fold_in(key, 5), 2, max(NB // 3, 1))
    second = symmetric_mask(jax.random.fold_in(key, 6), 2, max(NB // 3, 1))
    return jnp.stack([first, second])


def draw_density(key, part):
    key = jax.random.fold_in(key, 3)
    size = NB * BS
    scale = 1.0 / size ** 0.5
    noise = jax.random.normal(key, (size, size), jnp.float32)
    mixed = (noise + noise.T) * 0.70710678 * scale + 0.5 * jnp.eye(size, dtype=jnp.float32)
    return mixed.astype(jnp.bfloat16)


def setup_inputs(seed: int = 0) -> dict:
    streams_of = jax.random.split(jax.random.key(seed), 4)
    density = draw_density(jax.random.fold_in(streams_of[3], 71), 0)
    pattern = draw_pattern(jax.random.fold_in(streams_of[3], 71), 0)
    keep = draw_keep(jax.random.fold_in(streams_of[3], 71), 0)
    return {"density": density, "pattern": pattern, "keep": keep}


def expand(mask):
    return jnp.repeat(jnp.repeat(mask, BS, axis=0), BS, axis=1) > 0


def reference(density, pattern, keep):
    current = jnp.where(expand(pattern), density, jnp.zeros_like(density)).astype(jnp.bfloat16)
    for step in range(2):
        square = jnp.dot(current, current, preferred_element_type=jnp.float32)
        before = current.astype(jnp.float32)
        if step == 1:
            updated = 2.0 * before - square
        else:
            updated = square
        updated = jnp.where(expand(keep[step]), updated, jnp.zeros_like(updated))
        current = updated.astype(jnp.bfloat16)
    return current
```

```python
import functools

import jax
import jax.numpy as jnp
from jax import lax
from jax.experimental import pallas as pl
from jax.experimental.pallas import tpu as pltpu
from jax.sharding import PartitionSpec as P

BS = 128
NX, NY, NZ = 4, 4, 8
H = 384
CH = 96
MESH = pl.DeviceIdType.MESH

ORDER = [
    (0, 0), (1, 0), (3, 0), (0, 1), (0, 3), (3, 3), (3, 1), (1, 3),
    (1, 1), (2, 0), (0, 2), (3, 2), (2, 3), (1, 2), (2, 1), (2, 2),
]
SLOT = {place: i for i, place in enumerate(ORDER)}


def queues():
    along, back = [], []
    for queue, behind, keep in ((along, 3, 0), (back, 1, 1)):
        pair = (0, 1) if keep == 0 else (1, 0)
        first = [((0, 0), c) for c in pair]
        own = [((0, 0), 2 + c) for c in pair]
        queue += first + own
        queue += [((behind, 0), keep)]
        for other in (3, 1):
            queue += [((0, other), 2 + c) for c in pair]
        queue += [((behind, 0), 2 + keep)]
        queue += [((0, 2), 2 + c) for c in pair]
        queue += [((behind, other), 2 + keep) for other in (3, 1, 2)]

    def swapped(queue):
        return [((dy, dx), (c + 2) % 4) for (dx, dy), c in queue]

    up = [(0, c) for c in range(4)] + [(7, c) for c in range(4)]
    up += [(6, c) for c in range(4)] + [(5, c) for c in (0, 1)]
    down = [(0, c) for c in (3, 2, 1, 0)] + [(1, c) for c in (3, 2, 1, 0)]
    down += [(2, c) for c in (3, 2, 1, 0)] + [(3, c) for c in (3, 2)]
    return [along, back, swapped(along), swapped(back), up, down]


QUEUES = queues()

STAGES = [
    (9, 5, 1, 0),
    (11, 6, 1, 1),
    (13, 9, 2, 1),
    (15, 11, 2, 2),
    (16, 11, 3, 2),
    (17, 13, 3, 3),
    (18, 15, 4, 3),
    (19, 16, 4, 4),
]


def kernel(pattern, keep, density, out, a0, a1, b0, b1, acc, own,
           recv_a, recv_b, recv_c, send, misc):
    z = lax.axis_index("row")
    col = lax.axis_index("col")
    r = lax.axis_index("rep")
    x, y = col // NY, col % NY

    def at(dx, dy, dz):
        return ((z + dz) % NZ, ((x + dx) % NX) * NY + (y + dy) % NY, r)

    targets = [at(1, 0, 0), at(3, 0, 0), at(0, 1, 0), at(0, 3, 0), at(0, 0, 1), at(0, 0, 7)]
    other_core = (z, col, 1 - r)
    half = pl.ds(pl.multiple_of(r * H, H), H)

    load = pltpu.make_async_copy(density.at[half], own, misc.at[0])
    load.start()
    barrier = pltpu.get_barrier_semaphore()
    for target in targets + [other_core]:
        pl.semaphore_signal(barrier, inc=1, device_id=target, device_id_type=MESH)
    load.wait()

    def masked_store(mask, value, stores):
        for i in range(3):
            rows = slice(i * BS, (i + 1) * BS)
            for j in range(3):
                cols = slice(j * BS, (j + 1) * BS)
                kept = mask(z * 6 + r * 3 + i, col * 3 + j) > 0
                block = value(rows, cols)
                block = jnp.where(kept, block, jnp.zeros_like(block)).astype(jnp.bfloat16)
                for store in stores:
                    store[rows, cols] = block

    masked_store(
        lambda i, j: pattern[i, j], lambda rows, cols: own[rows, cols], [a0.at[0], b0.at[0, r]]
    )
    pl.semaphore_wait(barrier, 7)

    for step, (a, b) in enumerate(((a0, b0), (a1, b1))):
        waited = set()

        def dst_place(direction, place):
            if direction < 4:
                dx, dy = place
                shift = ((3, 0), (1, 0), (0, 3), (0, 1))[direction]
                return ((dx + shift[0]) % 4, (dy + shift[1]) % 4)
            return (place + (7, 1)[direction - 4]) % 8

        def piece_a(place, chunk):
            return a.at[SLOT[place], pl.ds(chunk * CH, CH)]

        def piece_b(place, chunk):
            return b.at[place, r, pl.ds(chunk * CH, CH)]

        def ensure_a(place, chunk):
            if place == (0, 0) or ("a", place, chunk) in waited:
                return
            waited.add(("a", place, chunk))
            ref = piece_a(place, chunk)
            pltpu.make_async_copy(ref, ref, recv_a.at[step, SLOT[place], chunk]).wait()

        def ensure_b(place, chunk):
            if place == 0 or ("b", place, chunk) in waited:
                return
            waited.add(("b", place, chunk))
            ref = piece_b(place, chunk)
            pltpu.make_async_copy(ref, ref, recv_b.at[step, place, chunk]).wait()

        def ensure_c(place):
            if ("c", place) in waited:
                return
            waited.add(("c", place))
            ref = b.at[place, 1 - r]
            pltpu.make_async_copy(ref, ref, recv_c.at[step, place]).wait()

        def share(place):
            if ("s", place) in waited:
                return
            waited.add(("s", place))
            pltpu.make_async_remote_copy(
                src_ref=b.at[place, r], dst_ref=b.at[place, r],
                send_sem=send.at[step, 6], recv_sem=recv_c.at[step, place],
                device_id=other_core, device_id_type=MESH,
            ).start()

        def issue(k):
            for direction, queue in enumerate(QUEUES):
                if k >= len(queue):
                    continue
                place, chunk = queue[k]
                if direction < 4:
                    ensure_a(place, chunk)
                    src = piece_a(place, chunk)
                    there = dst_place(direction, place)
                    dst = piece_a(there, chunk)
                    sem = recv_a.at[step, SLOT[there], chunk]
                else:
                    ensure_b(place, chunk)
                    src = piece_b(place, chunk)
                    there = dst_place(direction, place)
                    dst = piece_b(there, chunk)
                    sem = recv_b.at[step, there, chunk]
                pltpu.make_async_remote_copy(
                    src_ref=src, dst_ref=dst, send_sem=send.at[step, direction], recv_sem=sem,
                    device_id=targets[direction], device_id_type=MESH,
                ).start()

        def products(tiles, mine, shared, before):
            tiles0, mine0, shared0 = before

            def body(i, carry):
                dx, dy = jnp.int32(0), jnp.int32(0)
                for j, place in enumerate(ORDER[:tiles]):
                    if place != (0, 0):
                        dx = jnp.where(i == j, place[0], dx)
                        dy = jnp.where(i == j, place[1], dy)
                panel = ((x + dx) % NX) * NY + (y + dy) % NY
                rp = panel % 2
                dz = (panel // 2 + NZ - z) % NZ
                far = jnp.where(dz > 4, NZ - dz, dz)
                reach = jnp.where(rp == r, mine, shared)
                reach0 = jnp.where(rp == r, mine0, shared0)
                ready = jnp.where(far <= reach, 1, 0)
                done = jnp.where((i < tiles0) & (far <= reach0), 1, 0)

                @pl.when(ready > done)
                def _():
                    acc[...] += jnp.dot(a[i], b[dz, rp], preferred_element_type=jnp.float32)

                return carry

            lax.fori_loop(0, tiles, body, 0)

        for k in range(4):
            issue(k)
        share(0)
        acc[...] = jnp.zeros_like(acc)

        stages = list(STAGES)
        before = (0, -1, -1)
        for k in range(4, 20):
            if k < 15:
                issue(k)
            for near in range(1, 5):
                for place in {near, NZ - near}:
                    if all(("b", place, c) in waited for c in range(4)):
                        share(place)
            if stages and stages[0][0] == k + 1 or k >= 15 and stages:
                _, tiles, mine, shared = stages.pop(0)
                for place in ORDER[:tiles]:
                    for c in range(4):
                        ensure_a(place, c)
                for near in range(1, mine + 1):
                    for place in sorted({near, NZ - near}):
                        for c in range(4):
                            ensure_b(place, c)
                        share(place)
                for near in range(0, shared + 1):
                    for place in sorted({near, (NZ - near) % NZ}):
                        ensure_c(place)
                if not stages:
                    for direction, queue in enumerate(QUEUES):
                        n = len(queue)
                        ref = a.at[pl.ds(0, n), pl.ds(0, CH)]
                        pltpu.make_async_copy(ref, ref, send.at[step, direction]).wait()
                    ref = b.at[:, 0]
                    pltpu.make_async_copy(ref, ref, send.at[step, 6]).wait()
                products(tiles, mine, shared, before)
                before = (tiles, mine, shared)

        if step == 0:
            masked_store(
                lambda i, j: keep[0, i, j], lambda rows, cols: acc[rows, cols],
                [a1.at[0], b1.at[0, r]],
            )
        else:
            masked_store(
                lambda i, j: keep[1, i, j],
                lambda rows, cols: 2.0 * a[0, rows, cols].astype(jnp.float32) - acc[rows, cols],
                [own],
            )
    remote = pltpu.make_async_remote_copy(
        src_ref=own, dst_ref=out.at[half], send_sem=misc.at[1], recv_sem=misc.at[2],
        device_id=other_core, device_id_type=MESH,
    )
    remote.start()
    local = pltpu.make_async_copy(own, out.at[half], misc.at[0])
    local.start()
    local.wait()
    remote.wait()


def shards(density, pattern, keep):
    smem = pl.BlockSpec(memory_space=pltpu.SMEM)
    hbm = pl.BlockSpec(memory_space=pl.ANY)
    bf16 = jnp.bfloat16
    return pl.pallas_call(
        kernel,
        out_shape=jax.ShapeDtypeStruct(density.shape, bf16),
        in_specs=[smem, smem, hbm],
        out_specs=hbm,
        scratch_shapes=[
            pltpu.VMEM((16, H, H), bf16),
            pltpu.VMEM((16, H, H), bf16),
            pltpu.VMEM((NZ, 2, H, H), bf16),
            pltpu.VMEM((NZ, 2, H, H), bf16),
            pltpu.VMEM((H, H), jnp.float32),
            pltpu.VMEM((H, H), bf16),
            pltpu.SemaphoreType.DMA((2, 16, 4)),
            pltpu.SemaphoreType.DMA((2, NZ, 4)),
            pltpu.SemaphoreType.DMA((2, NZ)),
            pltpu.SemaphoreType.DMA((2, 7)),
            pltpu.SemaphoreType.DMA((3,)),
        ],
        name="purify",
        cost_estimate=pl.CostEstimate(flops=2 * 2 * H * H * 6144, bytes_accessed=2 * 768 * H * 2, transcendentals=0),
        compiler_params=pltpu.CompilerParams(
            collective_id=0, has_side_effects=True, vmem_limit_bytes=48 * 2**20
        ),
    )(pattern, keep, density)


def solution(mesh):
    in_specs = (P("row", "col"), P(), P())
    out_specs = P("row", "col")
    return jax.shard_map(shards, mesh=mesh, in_specs=in_specs, out_specs=out_specs, check_vma=False)
```

```python
import functools

import jax
import jax.numpy as jnp
from jax import lax
from jax.experimental import pallas as pl
from jax.experimental.pallas import tpu as pltpu
from jax.sharding import PartitionSpec as P

BS = 128
NX, NY, NZ = 4, 4, 8
H = 384
CH = 96
MESH = pl.DeviceIdType.MESH

ORDER = [
    (0, 0), (1, 0), (3, 0), (0, 1), (0, 3), (3, 3), (3, 1), (1, 3),
    (1, 1), (2, 0), (0, 2), (3, 2), (2, 3), (1, 2), (2, 1), (2, 2),
]
SLOT = {place: i for i, place in enumerate(ORDER)}


def queues():
    along, back = [], []
    for queue, behind, keep in ((along, 3, 0), (back, 1, 1)):
        pair = (0, 1) if keep == 0 else (1, 0)
        first = [((0, 0), c) for c in pair]
        own = [((0, 0), 2 + c) for c in pair]
        queue += first + own
        queue += [((behind, 0), keep)]
        for other in (3, 1):
            queue += [((0, other), 2 + c) for c in pair]
        queue += [((behind, 0), 2 + keep)]
        queue += [((0, 2), 2 + c) for c in pair]
        queue += [((behind, other), 2 + keep) for other in (3, 1, 2)]

    def swapped(queue):
        return [((dy, dx), (c + 2) % 4) for (dx, dy), c in queue]

    up = [(0, c) for c in range(4)] + [(7, c) for c in range(4)]
    up += [(6, c) for c in range(4)] + [(5, c) for c in (0, 1)]
    down = [(0, c) for c in (3, 2, 1, 0)] + [(1, c) for c in (3, 2, 1, 0)]
    down += [(2, c) for c in (3, 2, 1, 0)] + [(3, c) for c in (3, 2)]
    return [along, back, swapped(along), swapped(back), up, down]


QUEUES = queues()

STAGES = [
    (8, 5, 1, 0),
    (10, 5, 1, 1),
    (11, 6, 1, 1),
    (12, 6, 2, 1),
    (13, 9, 2, 1),
    (14, 11, 2, 2),
    (16, 11, 3, 2),
    (17, 13, 3, 3),
    (18, 15, 4, 3),
    (19, 16, 4, 4),
]


def kernel(pattern_hbm, keep_hbm, density, out, a0, a1, b0, b1, acc, own, pattern, keep,
           recv_a, recv_b, recv_c, send, misc):
    z = lax.axis_index("row")
    col = lax.axis_index("col")
    r = lax.axis_index("rep")
    x, y = col // NY, col % NY

    def at(dx, dy, dz):
        return ((z + dz) % NZ, ((x + dx) % NX) * NY + (y + dy) % NY, r)

    targets = [at(1, 0, 0), at(3, 0, 0), at(0, 1, 0), at(0, 3, 0), at(0, 0, 1), at(0, 0, 7)]
    other_core = (z, col, 1 - r)
    half = pl.ds(pl.multiple_of(r * H, H), H)

    load = pltpu.make_async_copy(density.at[half], own, misc.at[0])
    load.start()
    load_pattern = pltpu.make_async_copy(pattern_hbm, pattern, misc.at[1])
    load_pattern.start()
    load_keep = pltpu.make_async_copy(keep_hbm, keep, misc.at[2])
    load_keep.start()
    barrier = pltpu.get_barrier_semaphore()
    for target in targets + [other_core]:
        pl.semaphore_signal(barrier, inc=1, device_id=target, device_id_type=MESH)
    slot_of = []
    for dz in range(NZ):
        for shared in range(2):
            panel = ((z + dz) % NZ) * 2 + (1 - r if shared else r)
            dx, dy = (panel // NY + NX - x) % NX, (panel % NY + NY - y) % NY
            place = dx * NY + dy
            slot = jnp.int32(0)
            for j, (px, py) in enumerate(ORDER):
                slot = jnp.where(place == px * NY + py, j, slot)
            slot_of.append(slot)
    load_pattern.wait()
    load.wait()

    def masked_store(mask, value, stores):
        for i in range(3):
            rows = slice(i * BS, (i + 1) * BS)
            for j in range(3):
                cols = slice(j * BS, (j + 1) * BS)
                kept = mask(z * 6 + r * 3 + i, col * 3 + j) > 0
                block = value(rows, cols)
                block = jnp.where(kept, block, jnp.zeros_like(block)).astype(jnp.bfloat16)
                for store in stores:
                    store[rows, cols] = block

    masked_store(
        lambda i, j: pattern[i, j], lambda rows, cols: own[rows, cols], [a0.at[0], b0.at[0, r]]
    )
    pl.semaphore_wait(barrier, 7)

    for step, (a, b) in enumerate(((a0, b0), (a1, b1))):
        waited = set()

        def dst_place(direction, place):
            if direction < 4:
                dx, dy = place
                shift = ((3, 0), (1, 0), (0, 3), (0, 1))[direction]
                return ((dx + shift[0]) % 4, (dy + shift[1]) % 4)
            return (place + (7, 1)[direction - 4]) % 8

        def piece_a(place, chunk):
            return a.at[SLOT[place], pl.ds(chunk * CH, CH)]

        def piece_b(place, chunk):
            return b.at[place, r, pl.ds(chunk * CH, CH)]

        def ensure_a(place, chunk):
            if place == (0, 0) or ("a", place, chunk) in waited:
                return
            waited.add(("a", place, chunk))
            ref = piece_a(place, chunk)
            pltpu.make_async_copy(ref, ref, recv_a.at[step, SLOT[place], chunk]).wait()

        def ensure_b(place, chunk):
            if place == 0 or ("b", place, chunk) in waited:
                return
            waited.add(("b", place, chunk))
            ref = piece_b(place, chunk)
            pltpu.make_async_copy(ref, ref, recv_b.at[step, place, chunk]).wait()

        def ensure_c(place):
            if ("c", place) in waited:
                return
            waited.add(("c", place))
            ref = b.at[place, 1 - r]
            pltpu.make_async_copy(ref, ref, recv_c.at[step, place]).wait()

        def share(place):
            if ("s", place) in waited:
                return
            waited.add(("s", place))
            pltpu.make_async_remote_copy(
                src_ref=b.at[place, r], dst_ref=b.at[place, r],
                send_sem=send.at[step, 6], recv_sem=recv_c.at[step, place],
                device_id=other_core, device_id_type=MESH,
            ).start()

        def issue(k):
            for direction, queue in enumerate(QUEUES):
                if k >= len(queue):
                    continue
                place, chunk = queue[k]
                if direction < 4:
                    ensure_a(place, chunk)
                    src = piece_a(place, chunk)
                    there = dst_place(direction, place)
                    dst = piece_a(there, chunk)
                    sem = recv_a.at[step, SLOT[there], chunk]
                else:
                    ensure_b(place, chunk)
                    src = piece_b(place, chunk)
                    there = dst_place(direction, place)
                    dst = piece_b(there, chunk)
                    sem = recv_b.at[step, there, chunk]
                pltpu.make_async_remote_copy(
                    src_ref=src, dst_ref=dst, send_sem=send.at[step, direction], recv_sem=sem,
                    device_id=targets[direction], device_id_type=MESH,
                ).start()

        def products(tiles, mine, shared, before):
            tiles0, mine0, shared0 = before
            items = []
            for i in range(tiles0, tiles):
                dx, dy = ORDER[i]
                panel = ((x + dx) % NX) * NY + (y + dy) % NY
                rp = panel % 2
                dz = (panel // 2 + NZ - z) % NZ
                far = jnp.where(dz > 4, NZ - dz, dz)
                reach = jnp.where(rp == r, mine, shared)
                items.append((jnp.int32(i), dz, rp, jnp.where(far <= reach, 1, 0)))
            for reach0, reach, other in ((mine0, mine, 0), (shared0, shared, 1)):
                for near in range(reach0 + 1, reach + 1):
                    for dz in sorted({near, (NZ - near) % NZ}):
                        slot = slot_of[dz * 2 + other]
                        rp = 1 - r if other else r
                        items.append((slot, jnp.int32(dz), rp, jnp.where(slot < tiles0, 1, 0)))

            def body(n, carry):
                slot, dz, rp, ready = items[0]
                for m in range(1, len(items)):
                    slot, dz, rp, ready = [
                        jnp.where(n == m, new, old) for new, old in zip(items[m], (slot, dz, rp, ready))
                    ]

                @pl.when(ready > 0)
                def _():
                    acc[...] += jnp.dot(a[slot], b[dz, rp], preferred_element_type=jnp.float32)

                return carry

            if items:
                lax.fori_loop(0, len(items), body, 0)

        for k in range(4):
            issue(k)
        share(0)
        acc[...] = jnp.zeros_like(acc)

        stages = list(STAGES)
        before = (0, -1, -1)
        for k in range(4, 20):
            if k < 15:
                issue(k)
            for near in range(1, 5):
                for place in {near, NZ - near}:
                    if all(("b", place, c) in waited for c in range(4)):
                        share(place)
            if stages and stages[0][0] == k + 1 or k >= 15 and stages:
                _, tiles, mine, shared = stages.pop(0)
                for place in ORDER[:tiles]:
                    for c in range(4):
                        ensure_a(place, c)
                for near in range(1, mine + 1):
                    for place in sorted({near, NZ - near}):
                        for c in range(4):
                            ensure_b(place, c)
                        share(place)
                for near in range(0, shared + 1):
                    for place in sorted({near, (NZ - near) % NZ}):
                        ensure_c(place)
                products(tiles, mine, shared, before)
                before = (tiles, mine, shared)
                if len(stages) == 1:
                    for direction, queue in enumerate(QUEUES):
                        n = len(queue)
                        ref = a.at[pl.ds(0, n), pl.ds(0, CH)]
                        pltpu.make_async_copy(ref, ref, send.at[step, direction]).wait()
                    ref = b.at[:, 0]
                    pltpu.make_async_copy(ref, ref, send.at[step, 6]).wait()

        if step == 0:
            load_keep.wait()
            masked_store(
                lambda i, j: keep[0, i, j], lambda rows, cols: acc[rows, cols],
                [a1.at[0], b1.at[0, r]],
            )

    copies = []
    for i in range(3):
        rows = slice(i * BS, (i + 1) * BS)
        for j in range(3):
            cols = slice(j * BS, (j + 1) * BS)
            block = 2.0 * a1[0, rows, cols].astype(jnp.float32) - acc[rows, cols]
            kept = keep[1, z * 6 + r * 3 + i, col * 3 + j] > 0
            own[rows, cols] = jnp.where(kept, block, jnp.zeros_like(block)).astype(jnp.bfloat16)
        there = out.at[pl.ds(pl.multiple_of(r * H + i * BS, BS), BS)]
        remote = pltpu.make_async_remote_copy(
            src_ref=own.at[rows], dst_ref=there, send_sem=misc.at[3 + i], recv_sem=misc.at[6 + i],
            device_id=other_core, device_id_type=MESH,
        )
        remote.start()
        local = pltpu.make_async_copy(own.at[rows], there, misc.at[i])
        local.start()
        copies += [remote, local]
    for copy in copies:
        copy.wait()


def shards(density, pattern, keep):
    hbm = pl.BlockSpec(memory_space=pl.ANY)
    bf16 = jnp.bfloat16
    return pl.pallas_call(
        kernel,
        out_shape=jax.ShapeDtypeStruct(density.shape, bf16),
        in_specs=[hbm, hbm, hbm],
        out_specs=hbm,
        scratch_shapes=[
            pltpu.VMEM((16, H, H), bf16),
            pltpu.VMEM((16, H, H), bf16),
            pltpu.VMEM((NZ, 2, H, H), bf16),
            pltpu.VMEM((NZ, 2, H, H), bf16),
            pltpu.VMEM((H, H), jnp.float32),
            pltpu.VMEM((H, H), bf16),
            pltpu.SMEM(pattern.shape, jnp.int32),
            pltpu.SMEM(keep.shape, jnp.int32),
            pltpu.SemaphoreType.DMA((2, 16, 4)),
            pltpu.SemaphoreType.DMA((2, NZ, 4)),
            pltpu.SemaphoreType.DMA((2, NZ)),
            pltpu.SemaphoreType.DMA((2, 7)),
            pltpu.SemaphoreType.DMA((9,)),
        ],
        name="purify",
        cost_estimate=pl.CostEstimate(flops=2 * 2 * H * H * 6144, bytes_accessed=2 * 768 * H * 2, transcendentals=0),
        compiler_params=pltpu.CompilerParams(
            collective_id=0, has_side_effects=True, vmem_limit_bytes=60 * 2**20
        ),
    )(pattern, keep, density)


def solution(mesh):
    in_specs = (P("row", "col"), P(), P())
    out_specs = P("row", "col")
    return jax.shard_map(shards, mesh=mesh, in_specs=in_specs, out_specs=out_specs, check_vma=False)
```

```python
import jax
import jax.numpy as jnp
from jax import lax
from jax.experimental import pallas as pl
from jax.experimental.pallas import tpu as pltpu
from jax.sharding import PartitionSpec as P

BS = 128
NX, NY, NZ = 4, 4, 8
H = 384
CH = 96
HH = 192
Z_ROWS = (HH, CH)
WIDE = 256
FIRST_ROW = (0, 192, 96, 288)
COLS = (slice(0, WIDE), slice(WIDE, H))
GROUP = 2
MESH = pl.DeviceIdType.MESH

ORDER_UPPER = [
    (0, 0), (1, 0), (3, 0), (0, 1), (0, 3), (3, 3), (2, 0), (0, 2),
    (3, 2), (2, 3), (3, 1), (1, 3), (1, 1), (2, 2), (2, 1), (1, 2),
]
ORDER_REST = [
    (0, 0), (1, 0), (0, 1), (2, 0), (0, 2), (1, 1), (3, 0), (0, 3),
    (2, 1), (1, 2), (3, 2), (2, 3), (3, 1), (1, 3), (3, 3), (2, 2),
]
ORDER_LAST = [
    (0, 0), (1, 0), (3, 0), (0, 1), (0, 3), (3, 3), (3, 1), (1, 3),
    (1, 1), (2, 0), (0, 2), (3, 2), (2, 3), (1, 2), (2, 1), (2, 2),
]
ORDERS = [ORDER_UPPER, ORDER_REST, ORDER_LAST]

X_UP = [
    ((0, 0), 0), ((0, 0), 2), ((0, 0), 1), ((3, 0), 0), ((0, 3), 2), ((0, 1), 2), ((3, 0), 2), ((0, 2), 2),
    ((3, 3), 2), ((3, 1), 2), ((3, 2), 2), ((0, 0), 3), ((0, 2), 3), ((0, 1), 3), ((0, 3), 3),
]
X_DOWN = [
    ((0, 0), 0), ((0, 0), 2), ((0, 0), 1), ((0, 0), 3), ((1, 0), 1), ((0, 1), 3), ((0, 3), 3), ((1, 0), 3),
    ((0, 2), 3), ((0, 3), 2), ((0, 1), 2), ((0, 2), 2), ((1, 1), 3), ((1, 3), 3), ((1, 2), 3),
]
X_UP_LAST = [
    ((0, 0), 0), ((0, 0), 2), ((0, 0), 1), ((0, 0), 3), ((3, 0), 0), ((0, 3), 2), ((0, 3), 3), ((0, 1), 2),
    ((0, 1), 3), ((3, 0), 2), ((0, 2), 2), ((0, 2), 3), ((3, 3), 2), ((3, 1), 2), ((3, 2), 2),
]
X_DOWN_LAST = [
    ((0, 0), 0), ((0, 0), 2), ((0, 0), 1), ((0, 0), 3), ((1, 0), 1), ((0, 3), 3), ((0, 3), 2), ((0, 1), 3),
    ((0, 1), 2), ((1, 0), 3), ((0, 2), 3), ((0, 2), 2), ((1, 3), 3), ((1, 1), 3), ((1, 2), 3),
]


def swapped(queue):
    return [((dy, dx), (chunk + 2) % 4) for (dx, dy), chunk in queue]


Z_UP = [
    (0, 0, 0), (0, 0, 1), (0, 1, 0), (7, 0, 0), (7, 0, 1), (0, 1, 1), (6, 0, 0),
    (7, 1, 0), (6, 0, 1), (7, 1, 1), (6, 1, 0), (5, 0, 0), (6, 1, 1), (5, 1, 0),
]
Z_DOWN = [
    (0, 0, 0), (0, 0, 1), (0, 1, 1), (1, 0, 1), (1, 0, 0), (0, 1, 0), (2, 0, 1),
    (1, 1, 1), (2, 0, 0), (1, 1, 0), (2, 1, 1), (3, 0, 1), (2, 1, 0), (3, 1, 1),
]
Z_UP_LAST = [(dz, 0, chunk) for dz in (0, 7, 6) for chunk in range(4)] + [(5, 0, 0), (5, 0, 1)]
Z_DOWN_LAST = [(dz, 0, chunk) for dz in (0, 1, 2) for chunk in (3, 2, 1, 0)] + [(3, 0, 3), (3, 0, 2)]
QUEUES = [
    [X_UP, X_DOWN, swapped(X_UP), swapped(X_DOWN), Z_UP, Z_DOWN],
    [X_UP_LAST, X_DOWN_LAST, swapped(X_UP_LAST), swapped(X_DOWN_LAST), Z_UP_LAST, Z_DOWN_LAST],
]

STAGES = [
    [
        (8, 0, 5, 1, 1),
        (10, 0, 6, 2, 1),
        (10, 1, 3, 1, 0),
        (11, 0, 8, 2, 2),
        (13, 0, 12, 3, 2),
        (13, 1, 5, 2, 1),
        (15, 0, 14, 3, 3),
        (15, 1, 6, 2, 2),
        (15, 0, 16, 4, 3),
        (15, 1, 8, 2, 2),
        (15, 1, 10, 3, 2),
        (15, 0, 16, 4, 4),
        (15, 1, 14, 4, 3),
        (15, 1, 16, 4, 4),
    ],
    [
        (8, 2, 5, 1, 0),
        (10, 2, 5, 1, 1),
        (11, 2, 6, 1, 1),
        (12, 2, 6, 2, 1),
        (13, 2, 9, 2, 1),
        (14, 2, 11, 2, 2),
        (15, 2, 11, 3, 2),
        (15, 2, 13, 3, 3),
        (15, 2, 15, 4, 3),
        (15, 2, 16, 4, 4),
    ],
]


def kernel(pattern_hbm, keep_hbm, density, out, a0, a1, wide0, slim0, b1, acc, own, pattern, keep,
           recv_a, recv_b, recv_c, send, misc):
    z = lax.axis_index("row")
    col = lax.axis_index("col")
    r = lax.axis_index("rep")
    x, y = col // NY, col % NY

    def at(dx, dy, dz):
        return ((z + dz) % NZ, ((x + dx) % NX) * NY + (y + dy) % NY, r)

    targets = [at(1, 0, 0), at(3, 0, 0), at(0, 1, 0), at(0, 3, 0), at(0, 0, 1), at(0, 0, 7)]
    other_core = (z, col, 1 - r)

    barrier = pltpu.get_barrier_semaphore()
    for target in targets + [other_core]:
        pl.semaphore_signal(barrier, inc=1, device_id=target, device_id_type=MESH)
    load = pltpu.make_async_copy(density.at[pl.ds(pl.multiple_of(r * H, H), H)], own, misc.at[0])
    load.start()
    load_pattern = pltpu.make_async_copy(pattern_hbm, pattern, misc.at[1])
    load_pattern.start()
    load_keep = pltpu.make_async_copy(keep_hbm, keep, misc.at[2])
    load_keep.start()

    meets = []
    for dz in range(NZ):
        for other in range(2):
            panel = ((z + dz) % NZ) * 2 + (1 - r if other else r)
            place = ((panel // NY + NX - x) % NX) * NY + (panel % NY + NY - y) % NY
            ranks = []
            for order in ORDERS:
                rank = jnp.int32(0)
                for j, (px, py) in enumerate(order):
                    rank = jnp.where(place == px * NY + py, j, rank)
                ranks.append(rank)
            meets.append((place, ranks))
    load_pattern.wait()
    load.wait()

    def masked_store(mask, value, store, rows, cols):
        row = rows.start
        while row < rows.stop:
            row_end = min(rows.stop, (row // BS + 1) * BS)
            for j in range(cols.start // BS, cols.stop // BS):
                kept = mask(z * 6 + r * 3 + row // BS, col * 3 + j) > 0
                here, there = slice(row, row_end), slice(j * BS, (j + 1) * BS)
                block = value(here, there)
                store(here, there, jnp.where(kept, block, jnp.zeros_like(block)).astype(jnp.bfloat16))
            row = row_end

    def store_first(rows, cols, block):
        a0[0, rows, cols] = block
        if cols.start < WIDE:
            wide0[0, r, rows, cols] = block
        else:
            slim0[0, r, rows, slice(cols.start - WIDE, cols.stop - WIDE)] = block

    def store_second(rows, cols, block):
        a1[0, rows, cols] = block
        b1[0, r, rows, cols] = block

    def remote(src, dst, send_sem, recv_sem, target):
        pltpu.make_async_remote_copy(
            src_ref=src, dst_ref=dst, send_sem=send_sem, recv_sem=recv_sem,
            device_id=target, device_id_type=MESH,
        ).start()

    def arrived(ref, sem):
        pltpu.make_async_copy(ref, ref, sem).wait()

    def there_of(direction, place):
        if direction < 4:
            shift = ((3, 0), (1, 0), (0, 3), (0, 1))[direction]
            return ((place[0] + shift[0]) % NX, (place[1] + shift[1]) % NY)
        return (place + (7, 1)[direction - 4]) % NZ

    def slot_of(place):
        return place[0] * NY + place[1]

    def chunk_rows(chunk):
        return pl.ds(FIRST_ROW[chunk], CH)

    def send_chunk(step, a, direction, place, chunk, cols):
        there = there_of(direction, place)
        remote(
            a.at[slot_of(place), chunk_rows(chunk), cols], a.at[slot_of(there), chunk_rows(chunk), cols],
            send.at[step, direction], recv_a.at[step, slot_of(there), chunk], targets[direction],
        )

    def send_piece(step, b, direction, place, part, chunk, cols=None):
        there = there_of(direction, place)
        rows = pl.ds(chunk * Z_ROWS[step], Z_ROWS[step])
        src, dst = b.at[place, r, rows], b.at[there, r, rows]
        if cols is not None:
            src, dst = b.at[place, r, rows, cols], b.at[there, r, rows, cols]
        remote(src, dst, send.at[step, direction], recv_b.at[step, there, part, chunk], targets[direction])

    def send_early(step, a):
        for chunks, directions in (((0, 2), (0, 1)), ((2, 0), (2, 3))):
            for chunk in chunks:
                for direction in directions:
                    send_chunk(step, a, direction, (0, 0), chunk, pl.ds(0, WIDE))
        for direction in (4, 5):
            if step == 0:
                send_piece(step, wide0, direction, 0, 0, 0)
            else:
                for chunk in (0, 1):
                    send_piece(step, b1, direction, 0, 0, chunk, pl.ds(0, WIDE))

    upper, lower, full = slice(0, HH), slice(HH, H), slice(0, H)
    masked = lambda rows, cols: masked_store(
        lambda i, j: pattern[i, j], lambda i, j: own[i, j], store_first, rows, cols
    )
    masked(upper, COLS[0])
    pl.semaphore_wait(barrier, 7)
    send_early(0, a0)
    masked(upper, COLS[1])
    masked(lower, full)

    for step, (a, parts) in enumerate(((a0, (wide0, slim0)), (a1, (b1,)))):
        waited = set()

        def once(*key):
            if key in waited:
                return False
            waited.add(key)
            return True

        def ensure_a(place, chunk):
            if place != (0, 0) and once("a", place, chunk):
                arrived(a.at[slot_of(place), chunk_rows(chunk)], recv_a.at[step, slot_of(place), chunk])

        def ensure_b(place, part, chunk):
            if place != 0 and once("b", place, part, chunk):
                arrived(parts[part].at[place, r, pl.ds(chunk * Z_ROWS[step], Z_ROWS[step])], recv_b.at[step, place, part, chunk])

        def ensure_c(place, part):
            if once("c", place, part):
                arrived(parts[part].at[place, 1 - r], recv_c.at[step, place, part])

        def share(place, part):
            if once("s", place, part):
                ref = parts[part].at[place, r]
                remote(ref, ref, send.at[step, 6], recv_c.at[step, place, part], other_core)

        def issue(k):
            for direction, queue in enumerate(QUEUES[step]):
                if k >= len(queue):
                    continue
                rest = pl.ds(WIDE, H - WIDE)
                if direction < 4:
                    place, chunk = queue[k]
                    ensure_a(place, chunk)
                    early = place == (0, 0) and chunk in (0, 2)
                    send_chunk(step, a, direction, place, chunk, rest if early else pl.ds(0, H))
                else:
                    place, part, chunk = queue[k]
                    ensure_b(place, part, chunk)
                    if step == 1:
                        send_piece(step, b1, direction, place, 0, chunk, rest if place == 0 and chunk < 2 else None)
                    elif (place, part, chunk) != (0, 0, 0):
                        send_piece(step, parts[part], direction, place, part, chunk)
            for place in range(1, NZ):
                for part in range(len(parts)):
                    if all(("b", place, part, chunk) in waited for chunk in range(H // Z_ROWS[step])):
                        share(place, part)

        def products(region, count, mine, shared, before):
            count0, mine0, shared0 = before
            order = ORDERS[region]
            items = []
            for i in range(count0, count):
                dx, dy = order[i]
                panel = ((x + dx) % NX) * NY + (y + dy) % NY
                rp = panel % 2
                dz = (panel // 2 + NZ - z) % NZ
                far = jnp.where(dz > 4, NZ - dz, dz)
                reach = jnp.where(rp == r, mine, shared)
                items.append((jnp.int32(slot_of((dx, dy))), dz, rp, jnp.where(far <= reach, 1, 0)))
            for reach0, reach, other in ((mine0, mine, 0), (shared0, shared, 1)):
                for near in range(reach0 + 1, reach + 1):
                    for dz in sorted({near, (NZ - near) % NZ}):
                        place, ranks = meets[dz * 2 + other]
                        rp = 1 - r if other else r
                        items.append((place, jnp.int32(dz), rp, jnp.where(ranks[region] < count0, 1, 0)))

            if not items:
                return
            total, picks = jnp.int32(0), []
            for slot, dz, rp, ready in items:
                picks.append((jnp.where(ready > 0, total, -1), slot * 16 + dz * 2 + rp))
                total = total + ready

            def add(first, size):
                sums = {}
                for n in range(size):
                    code = jnp.int32(0)
                    for rank, item in picks:
                        code = jnp.where(rank == first + n, item, code)
                    slot, dz, rp = code // 16, code // 2 % NZ, code % 2
                    if region == 0:
                        terms = [(upper, COLS[0], wide0)]
                    elif region == 1:
                        terms = [(lower, COLS[0], wide0), (full, COLS[1], slim0)]
                    else:
                        terms = [(full, full, b1)]
                    for rows, cols, b in terms:
                        term = jnp.dot(a[slot, rows], b[dz, rp], preferred_element_type=jnp.float32)
                        key = (rows.start, rows.stop, cols.start, cols.stop)
                        sums[key] = sums[key] + term if key in sums else term
                for (r0, r1, c0, c1), term in sums.items():
                    acc[r0:r1, c0:c1] += term

            size = GROUP
            while size > len(items):
                size //= 2

            @pl.loop(0, total // size)
            def _(j):
                add(j * size, size)

            while size > 1:
                size //= 2

                @pl.when(total // size % 2 == 1)
                def _():
                    add(total // (2 * size) * (2 * size), size)

        issue(0)
        issue(1)
        for part in range(len(parts)):
            share(0, part)
        issue(2)
        acc[...] = jnp.zeros_like(acc)

        before = [(0, -1, -1)] * 3
        stages = list(STAGES[step])
        for k in range(3, 15):
            issue(k)
            while stages and stages[0][0] == k + 1:
                _, region, count, mine, shared = stages.pop(0)
                needed = range(1 if region == 0 else len(parts))
                for place in ORDERS[region][:count]:
                    for chunk in (0, 2) if region == 0 else (0, 1, 2, 3):
                        ensure_a(place, chunk)
                for near in range(0, mine + 1):
                    for dz in sorted({near, (NZ - near) % NZ}):
                        for part in needed:
                            for chunk in range(H // Z_ROWS[step]):
                                ensure_b(dz, part, chunk)
                            share(dz, part)
                for near in range(0, shared + 1):
                    for dz in sorted({near, (NZ - near) % NZ}):
                        for part in needed:
                            ensure_c(dz, part)
                if not stages:
                    for direction, queue in enumerate(QUEUES[step]):
                        arrived(a.at[pl.ds(0, len(queue)), pl.ds(0, CH)], send.at[step, direction])
                    arrived(a.at[pl.ds(0, NZ)], send.at[step, 6])
                products(region, count, mine, shared, before[region])
                before[region] = (count, mine, shared)
                if step == 0 and region == 0 and (count, mine, shared) == (16, 4, 4):
                    masked = lambda rows, cols: masked_store(
                        lambda i, j: keep[0, i, j], lambda i, j: acc[i, j], store_second, rows, cols
                    )
                    load_keep.wait()
                    masked(upper, COLS[0])
                    send_early(1, a1)

        if step == 0:
            masked(upper, COLS[1])
            masked(lower, full)

    copies = []
    for i in range(3):
        rows = slice(i * BS, (i + 1) * BS)
        there = pl.ds(pl.multiple_of(r * H + i * BS, BS), BS)
        for j in range(3):
            cols = slice(j * BS, (j + 1) * BS)
            block = 2.0 * a1[0, rows, cols].astype(jnp.float32) - acc[rows, cols]
            kept = keep[1, z * 6 + r * 3 + i, col * 3 + j] > 0
            out[there, cols] = jnp.where(kept, block, jnp.zeros_like(block)).astype(jnp.bfloat16)
        copy = pltpu.make_async_remote_copy(
            src_ref=out.at[there], dst_ref=out.at[there], send_sem=misc.at[3 + i], recv_sem=misc.at[6 + i],
            device_id=other_core, device_id_type=MESH,
        )
        copy.start()
        copies.append(copy)
    for copy in copies:
        copy.wait()


def shards(density, pattern, keep):
    hbm = pl.BlockSpec(memory_space=pl.ANY)
    bf16 = jnp.bfloat16
    return pl.pallas_call(
        kernel,
        out_shape=pltpu.VMEM(density.shape, bf16),
        in_specs=[hbm, hbm, hbm],
        out_specs=pl.BlockSpec(memory_space=pltpu.VMEM),
        scratch_shapes=[
            pltpu.VMEM((NX * NY, H, H), bf16),
            pltpu.VMEM((NX * NY, H, H), bf16),
            pltpu.VMEM((NZ, 2, H, WIDE), bf16),
            pltpu.VMEM((NZ, 2, H, H - WIDE), bf16),
            pltpu.VMEM((NZ, 2, H, H), bf16),
            pltpu.VMEM((H, H), jnp.float32),
            pltpu.VMEM((H, H), bf16),
            pltpu.SMEM(pattern.shape, jnp.int32),
            pltpu.SMEM(keep.shape, jnp.int32),
            pltpu.SemaphoreType.DMA((2, NX * NY, 4)),
            pltpu.SemaphoreType.DMA((2, NZ, 2, 4)),
            pltpu.SemaphoreType.DMA((2, NZ, 2)),
            pltpu.SemaphoreType.DMA((2, 7)),
            pltpu.SemaphoreType.DMA((9,)),
        ],
        name="purify",
        cost_estimate=pl.CostEstimate(flops=2 * 2 * H * H * 6144, bytes_accessed=2 * 768 * H * 2, transcendentals=0),
        compiler_params=pltpu.CompilerParams(
            collective_id=0, has_side_effects=True, vmem_limit_bytes=60 * 2**20
        ),
    )(pattern, keep, density)


def solution(mesh):
    in_specs = (P("row", "col"), P(), P())
    out_specs = P("row", "col")
    return jax.shard_map(shards, mesh=mesh, in_specs=in_specs, out_specs=out_specs, check_vma=False)
```

```python
import jax
import jax.numpy as jnp
from jax import lax
from jax.experimental import pallas as pl
from jax.experimental.pallas import tpu as pltpu
from jax.sharding import PartitionSpec as P

BS = 128
NX, NY, NZ = 4, 4, 8
H = 384
CH = 96
HH = 192
Z_ROWS = (HH, CH)
WIDE = 256
FIRST_ROW = (0, 192, 96, 288)
COLS = (slice(0, WIDE), slice(WIDE, H))
GROUP = 4
MESH = pl.DeviceIdType.MESH

ORDER_UPPER = [
    (0, 0), (1, 0), (3, 0), (0, 1), (0, 3), (3, 3), (1, 1), (3, 1),
    (1, 3), (2, 0), (0, 2), (3, 2), (2, 3), (2, 1), (1, 2), (2, 2),
]
ORDER_REST = [
    (0, 0), (1, 0), (3, 0), (0, 1), (0, 3), (1, 1), (2, 0), (0, 2),
    (2, 1), (1, 2), (3, 1), (1, 3), (2, 3), (3, 2), (2, 2), (3, 3),
]
ORDER_LAST = [
    (0, 0), (1, 0), (3, 0), (0, 1), (0, 3), (3, 3), (1, 3), (1, 1),
    (3, 1), (2, 0), (0, 2), (2, 3), (3, 2), (2, 1), (1, 2), (2, 2),
]
ORDERS = [ORDER_UPPER, ORDER_REST, ORDER_LAST]

X_UP = [
    ((0, 0), 0), ((0, 0), 2), ((0, 0), 1), ((0, 0), 3), ((3, 0), 0), ((0, 3), 2), ((0, 1), 2), ((3, 0), 2),
    ((0, 2), 2), ((3, 3), 2), ((3, 1), 2), ((3, 2), 2), ((0, 1), 3), ((0, 2), 3), ((0, 3), 3),
]
X_DOWN = [
    ((0, 0), 0), ((0, 0), 2), ((0, 0), 1), ((0, 0), 3), ((0, 3), 2), ((0, 1), 2), ((1, 0), 1), ((0, 1), 3),
    ((0, 3), 3), ((0, 2), 2), ((0, 2), 3), ((1, 0), 3), ((1, 1), 3), ((1, 3), 3), ((1, 2), 3),
]
X_UP_LAST = [
    ((0, 0), 0), ((0, 0), 2), ((0, 0), 1), ((0, 0), 3), ((3, 0), 0), ((0, 3), 2), ((0, 1), 2), ((0, 3), 3),
    ((0, 1), 3), ((3, 0), 2), ((0, 2), 2), ((0, 2), 3), ((3, 3), 2), ((3, 1), 2), ((3, 2), 2),
]
X_DOWN_LAST = [
    ((0, 0), 0), ((0, 0), 2), ((0, 0), 1), ((0, 0), 3), ((0, 3), 2), ((0, 1), 2), ((1, 0), 1), ((0, 3), 3),
    ((0, 1), 3), ((1, 0), 3), ((0, 2), 3), ((0, 2), 2), ((1, 3), 3), ((1, 1), 3), ((1, 2), 3),
]


def swapped(queue):
    return [((dy, dx), (chunk + 2) % 4) for (dx, dy), chunk in queue]


Z_UP = [
    (0, 0, 0), (0, 0, 1), (0, 1, 0), (0, 1, 1), (7, 0, 0), (7, 0, 1), (7, 1, 0),
    (7, 1, 1), (6, 0, 0), (6, 0, 1), (6, 1, 0), (5, 0, 0), (6, 1, 1), (5, 1, 0),
]
Z_DOWN = [((NZ - dz) % NZ, part, 1 - chunk) for dz, part, chunk in Z_UP]
Z_UP_LAST = [(dz, 0, chunk) for dz in (0, 7, 6) for chunk in range(4)] + [(5, 0, 0), (5, 0, 1)]
Z_DOWN_LAST = [
    (0, 0, 0), (0, 0, 1), (0, 0, 3), (0, 0, 2), (1, 0, 0), (1, 0, 3), (1, 0, 2),
    (1, 0, 1), (2, 0, 3), (2, 0, 2), (2, 0, 0), (2, 0, 1), (3, 0, 3), (3, 0, 2),
]
QUEUES = [
    [X_UP, X_DOWN, swapped(X_UP), swapped(X_DOWN), Z_UP, Z_DOWN],
    [X_UP_LAST, X_DOWN_LAST, swapped(X_UP_LAST), swapped(X_DOWN_LAST), Z_UP_LAST, Z_DOWN_LAST],
]

STAGES = [
    [
        (9, 0, 5, 1, 1),
        (10, 1, 5, 1, 1),
        (11, 0, 9, 2, 1),
        (12, 0, 11, 2, 2),
        (13, 1, 6, 2, 2),
        (14, 0, 13, 2, 2),
        (15, 0, 15, 3, 2),
        (15, 0, 16, 3, 3),
        (15, 1, 8, 2, 2),
        (15, 0, 16, 4, 3),
        (15, 1, 12, 2, 2),
        (15, 0, 16, 4, 4),
        (15, 1, 14, 4, 3),
        (15, 1, 16, 4, 4),
    ],
    [
        (9, 2, 5, 1, 0),
        (10, 2, 5, 1, 1),
        (12, 2, 6, 2, 1),
        (13, 2, 9, 2, 2),
        (14, 2, 11, 2, 2),
        (15, 2, 11, 3, 2),
        (15, 2, 13, 3, 3),
        (15, 2, 15, 4, 3),
        (15, 2, 16, 4, 4),
    ],
]


def kernel(pattern_hbm, keep_hbm, density, out, a0, a1, wide0, slim0, b1, acc, own, pattern, keep,
           recv_a, recv_b, recv_c, send, misc):
    z = lax.axis_index("row")
    col = lax.axis_index("col")
    r = lax.axis_index("rep")
    x, y = col // NY, col % NY

    def at(dx, dy, dz):
        return ((z + dz) % NZ, ((x + dx) % NX) * NY + (y + dy) % NY, r)

    targets = [at(1, 0, 0), at(3, 0, 0), at(0, 1, 0), at(0, 3, 0), at(0, 0, 1), at(0, 0, 7)]
    other_core = (z, col, 1 - r)

    barrier = pltpu.get_barrier_semaphore()
    for target in targets + [other_core]:
        pl.semaphore_signal(barrier, inc=1, device_id=target, device_id_type=MESH)
    load = pltpu.make_async_copy(density.at[pl.ds(pl.multiple_of(r * H, H), H)], own, misc.at[0])
    load.start()
    load_pattern = pltpu.make_async_copy(pattern_hbm, pattern, misc.at[1])
    load_pattern.start()
    load_keep = pltpu.make_async_copy(keep_hbm, keep, misc.at[2])
    load_keep.start()

    meets = []
    for dz in range(NZ):
        for other in range(2):
            panel = ((z + dz) % NZ) * 2 + (1 - r if other else r)
            place = ((panel // NY + NX - x) % NX) * NY + (panel % NY + NY - y) % NY
            ranks = []
            for order in ORDERS:
                rank = jnp.int32(0)
                for j, (px, py) in enumerate(order):
                    rank = jnp.where(place == px * NY + py, j, rank)
                ranks.append(rank)
            meets.append((place, ranks))
    load_pattern.wait()
    load.wait()

    def masked_store(mask, value, store, rows, cols):
        row = rows.start
        while row < rows.stop:
            row_end = min(rows.stop, (row // BS + 1) * BS)
            for j in range(cols.start // BS, cols.stop // BS):
                kept = mask(z * 6 + r * 3 + row // BS, col * 3 + j) > 0
                here, there = slice(row, row_end), slice(j * BS, (j + 1) * BS)
                block = value(here, there)
                store(here, there, jnp.where(kept, block, jnp.zeros_like(block)).astype(jnp.bfloat16))
            row = row_end

    def store_first(rows, cols, block):
        a0[0, rows, cols] = block
        if cols.start < WIDE:
            wide0[0, r, rows, cols] = block
        else:
            slim0[0, r, rows, slice(cols.start - WIDE, cols.stop - WIDE)] = block

    def store_second(rows, cols, block):
        a1[0, rows, cols] = block
        b1[0, r, rows, cols] = block

    def remote(src, dst, send_sem, recv_sem, target):
        pltpu.make_async_remote_copy(
            src_ref=src, dst_ref=dst, send_sem=send_sem, recv_sem=recv_sem,
            device_id=target, device_id_type=MESH,
        ).start()

    def arrived(ref, sem):
        pltpu.make_async_copy(ref, ref, sem).wait()

    def there_of(direction, place):
        if direction < 4:
            shift = ((3, 0), (1, 0), (0, 3), (0, 1))[direction]
            return ((place[0] + shift[0]) % NX, (place[1] + shift[1]) % NY)
        return (place + (7, 1)[direction - 4]) % NZ

    def slot_of(place):
        return place[0] * NY + place[1]

    def chunk_rows(chunk):
        return pl.ds(FIRST_ROW[chunk], CH)

    def send_chunk(step, a, direction, place, chunk, cols):
        there = there_of(direction, place)
        remote(
            a.at[slot_of(place), chunk_rows(chunk), cols], a.at[slot_of(there), chunk_rows(chunk), cols],
            send.at[step, direction], recv_a.at[step, slot_of(there), chunk], targets[direction],
        )

    def send_piece(step, b, direction, place, part, chunk, cols=None):
        there = there_of(direction, place)
        rows = pl.ds(chunk * Z_ROWS[step], Z_ROWS[step])
        src, dst = b.at[place, r, rows], b.at[there, r, rows]
        if cols is not None:
            src, dst = b.at[place, r, rows, cols], b.at[there, r, rows, cols]
        remote(src, dst, send.at[step, direction], recv_b.at[step, there, part, chunk], targets[direction])

    def send_early(step, a):
        for chunks, directions in (((0, 2), (0, 1)), ((2, 0), (2, 3))):
            for chunk in chunks:
                for direction in directions:
                    send_chunk(step, a, direction, (0, 0), chunk, pl.ds(0, WIDE))
        for direction in (4, 5):
            if step == 0 and direction == 4:
                send_piece(step, wide0, direction, 0, 0, 0)
            elif step == 1:
                for chunk in (0, 1):
                    send_piece(step, b1, direction, 0, 0, chunk, pl.ds(0, WIDE))

    upper, lower, full = slice(0, HH), slice(HH, H), slice(0, H)
    masked = lambda rows, cols: masked_store(
        lambda i, j: pattern[i, j], lambda i, j: own[i, j], store_first, rows, cols
    )
    masked(upper, COLS[0])
    pl.semaphore_wait(barrier, 7)
    send_early(0, a0)
    masked(upper, COLS[1])
    masked(lower, full)

    for step, (a, parts) in enumerate(((a0, (wide0, slim0)), (a1, (b1,)))):
        waited = set()

        def once(*key):
            if key in waited:
                return False
            waited.add(key)
            return True

        def ensure_a(place, chunk):
            if place != (0, 0) and once("a", place, chunk):
                arrived(a.at[slot_of(place), chunk_rows(chunk)], recv_a.at[step, slot_of(place), chunk])

        def ensure_b(place, part, chunk):
            if place != 0 and once("b", place, part, chunk):
                arrived(parts[part].at[place, r, pl.ds(chunk * Z_ROWS[step], Z_ROWS[step])], recv_b.at[step, place, part, chunk])

        def ensure_c(place, part):
            if once("c", place, part):
                arrived(parts[part].at[place, 1 - r], recv_c.at[step, place, part])

        def share(place, part):
            if once("s", place, part):
                ref = parts[part].at[place, r]
                remote(ref, ref, send.at[step, 6], recv_c.at[step, place, part], other_core)

        def issue(k):
            for direction, queue in enumerate(QUEUES[step]):
                if k >= len(queue):
                    continue
                rest = pl.ds(WIDE, H - WIDE)
                if direction < 4:
                    place, chunk = queue[k]
                    ensure_a(place, chunk)
                    early = place == (0, 0) and chunk in (0, 2)
                    send_chunk(step, a, direction, place, chunk, rest if early else pl.ds(0, H))
                else:
                    place, part, chunk = queue[k]
                    ensure_b(place, part, chunk)
                    if step == 1:
                        send_piece(step, b1, direction, place, 0, chunk, rest if place == 0 and chunk < 2 else None)
                    elif (direction, place, part, chunk) != (4, 0, 0, 0):
                        send_piece(step, parts[part], direction, place, part, chunk)
            for place in range(1, NZ):
                for part in range(len(parts)):
                    if all(("b", place, part, chunk) in waited for chunk in range(H // Z_ROWS[step])):
                        share(place, part)

        def products(region, count, mine, shared, before):
            count0, mine0, shared0 = before
            order = ORDERS[region]
            items = []
            for i in range(count0, count):
                dx, dy = order[i]
                panel = ((x + dx) % NX) * NY + (y + dy) % NY
                rp = panel % 2
                dz = (panel // 2 + NZ - z) % NZ
                far = jnp.where(dz > 4, NZ - dz, dz)
                reach = jnp.where(rp == r, mine, shared)
                items.append((jnp.int32(slot_of((dx, dy))), dz, rp, jnp.where(far <= reach, 1, 0)))
            for reach0, reach, other in ((mine0, mine, 0), (shared0, shared, 1)):
                for near in range(reach0 + 1, reach + 1):
                    for dz in sorted({near, (NZ - near) % NZ}):
                        place, ranks = meets[dz * 2 + other]
                        rp = 1 - r if other else r
                        items.append((place, jnp.int32(dz), rp, jnp.where(ranks[region] < count0, 1, 0)))

            if not items:
                return
            total, picks = jnp.int32(0), []
            for slot, dz, rp, ready in items:
                picks.append((jnp.where(ready > 0, total, -1), slot * 16 + dz * 2 + rp))
                total = total + ready

            def add(first, size):
                slots, halves = [], []
                for n in range(size):
                    code = jnp.int32(0)
                    for rank, item in picks:
                        code = jnp.where(rank == first + n, item, code)
                    slots.append(lax.div(code, 16))
                    halves.append((lax.rem(lax.div(code, 2), NZ), lax.rem(code, 2)))
                if region == 0:
                    terms = [(upper, COLS[0], wide0)]
                elif region == 1:
                    terms = [(lower, COLS[0], wide0), (full, COLS[1], slim0)]
                else:
                    terms = [(full, full, b1)]
                for rows, cols, b in terms:
                    left = jnp.concatenate([a[slot, rows] for slot in slots], axis=1)
                    right = jnp.concatenate([b[dz, rp] for dz, rp in halves], axis=0)
                    acc[rows, cols] += jnp.dot(left, right, preferred_element_type=jnp.float32)

            size = GROUP
            while size > len(items):
                size //= 2

            @pl.loop(0, total // size)
            def _(j):
                add(j * size, size)

            while size > 1:
                size //= 2

                @pl.when(total // size % 2 == 1)
                def _():
                    add(total // (2 * size) * (2 * size), size)

        issue(0)
        issue(1)
        for part in range(len(parts)):
            share(0, part)
        issue(2)
        acc[...] = jnp.zeros_like(acc)

        before = [(0, -1, -1)] * 3
        stages = list(STAGES[step])
        for k in range(3, 15):
            issue(k)
            while stages and stages[0][0] == k + 1:
                _, region, count, mine, shared = stages.pop(0)
                needed = range(1 if region == 0 else len(parts))
                for place in ORDERS[region][:count]:
                    for chunk in (0, 2) if region == 0 else (0, 1, 2, 3):
                        ensure_a(place, chunk)
                for near in range(0, mine + 1):
                    for dz in sorted({near, (NZ - near) % NZ}):
                        for part in needed:
                            for chunk in range(H // Z_ROWS[step]):
                                ensure_b(dz, part, chunk)
                            share(dz, part)
                for near in range(0, shared + 1):
                    for dz in sorted({near, (NZ - near) % NZ}):
                        for part in needed:
                            ensure_c(dz, part)
                if not stages:
                    for direction, queue in enumerate(QUEUES[step]):
                        arrived(a.at[pl.ds(0, len(queue)), pl.ds(0, CH)], send.at[step, direction])
                    arrived(a.at[pl.ds(0, NZ)], send.at[step, 6])
                products(region, count, mine, shared, before[region])
                before[region] = (count, mine, shared)
                if step == 0 and region == 0 and (count, mine, shared) == (16, 4, 4):
                    masked = lambda rows, cols: masked_store(
                        lambda i, j: keep[0, i, j], lambda i, j: acc[i, j], store_second, rows, cols
                    )
                    load_keep.wait()
                    masked(upper, COLS[0])
                    send_early(1, a1)

        if step == 0:
            masked(upper, COLS[1])
            masked(lower, full)

    copies = []
    for i in range(3):
        rows = slice(i * BS, (i + 1) * BS)
        there = pl.ds(pl.multiple_of(r * H + i * BS, BS), BS)
        for j in range(3):
            cols = slice(j * BS, (j + 1) * BS)
            block = 2.0 * a1[0, rows, cols].astype(jnp.float32) - acc[rows, cols]
            kept = keep[1, z * 6 + r * 3 + i, col * 3 + j] > 0
            out[there, cols] = jnp.where(kept, block, jnp.zeros_like(block)).astype(jnp.bfloat16)
        copy = pltpu.make_async_remote_copy(
            src_ref=out.at[there], dst_ref=out.at[there], send_sem=misc.at[3 + i], recv_sem=misc.at[6 + i],
            device_id=other_core, device_id_type=MESH,
        )
        copy.start()
        copies.append(copy)
    for copy in copies:
        copy.wait()


def shards(density, pattern, keep):
    hbm = pl.BlockSpec(memory_space=pl.ANY)
    bf16 = jnp.bfloat16
    return pl.pallas_call(
        kernel,
        out_shape=pltpu.VMEM(density.shape, bf16),
        in_specs=[hbm, hbm, hbm],
        out_specs=pl.BlockSpec(memory_space=pltpu.VMEM),
        scratch_shapes=[
            pltpu.VMEM((NX * NY, H, H), bf16),
            pltpu.VMEM((NX * NY, H, H), bf16),
            pltpu.VMEM((NZ, 2, H, WIDE), bf16),
            pltpu.VMEM((NZ, 2, H, H - WIDE), bf16),
            pltpu.VMEM((NZ, 2, H, H), bf16),
            pltpu.VMEM((H, H), jnp.float32),
            pltpu.VMEM((H, H), bf16),
            pltpu.SMEM(pattern.shape, jnp.int32),
            pltpu.SMEM(keep.shape, jnp.int32),
            pltpu.SemaphoreType.DMA((2, NX * NY, 4)),
            pltpu.SemaphoreType.DMA((2, NZ, 2, 4)),
            pltpu.SemaphoreType.DMA((2, NZ, 2)),
            pltpu.SemaphoreType.DMA((2, 7)),
            pltpu.SemaphoreType.DMA((9,)),
        ],
        name="purify",
        cost_estimate=pl.CostEstimate(flops=2 * 2 * H * H * 6144, bytes_accessed=2 * 768 * H * 2, transcendentals=0),
        compiler_params=pltpu.CompilerParams(
            collective_id=0, has_side_effects=True, vmem_limit_bytes=60 * 2**20
        ),
    )(pattern, keep, density)


def solution(mesh):
    in_specs = (P("row", "col"), P(), P())
    out_specs = P("row", "col")
    return jax.shard_map(shards, mesh=mesh, in_specs=in_specs, out_specs=out_specs, check_vma=False)
```

```python
import jax
import jax.numpy as jnp
from jax import lax
from jax.experimental import pallas as pl
from jax.experimental.pallas import tpu as pltpu
from jax.sharding import PartitionSpec as P

BS = 128
NX, NY, NZ = 4, 4, 8
H = 384
CH = 96
HH = 192
Z_ROWS = (HH, CH)
WIDE = 256
FIRST_ROW = (0, 192, 96, 288)
COLS = (slice(0, WIDE), slice(WIDE, H))
GROUP = 4
MESH = pl.DeviceIdType.MESH

ORDER_UPPER = [
    (0, 0), (1, 0), (3, 0), (0, 1), (0, 3), (3, 3), (1, 1), (3, 1),
    (1, 3), (2, 0), (0, 2), (3, 2), (2, 3), (2, 1), (1, 2), (2, 2),
]
ORDER_REST = [
    (0, 0), (1, 0), (3, 0), (0, 1), (0, 3), (1, 1), (2, 0), (0, 2),
    (2, 1), (1, 2), (3, 1), (1, 3), (2, 3), (3, 2), (2, 2), (3, 3),
]
ORDER_LAST = [
    (0, 0), (1, 0), (3, 0), (0, 1), (0, 3), (3, 3), (1, 3), (1, 1),
    (3, 1), (2, 0), (0, 2), (2, 3), (3, 2), (2, 1), (1, 2), (2, 2),
]
ORDERS = [ORDER_UPPER, ORDER_REST, ORDER_LAST]

X_UP = [
    ((0, 0), 0), ((0, 0), 2), ((0, 0), 1), ((0, 0), 3), ((3, 0), 0), ((0, 3), 2), ((0, 1), 2), ((3, 0), 2),
    ((0, 2), 2), ((3, 3), 2), ((3, 1), 2), ((3, 2), 2), ((0, 1), 3), ((0, 2), 3), ((0, 3), 3),
]
X_DOWN = [
    ((0, 0), 0), ((0, 0), 2), ((0, 0), 1), ((0, 0), 3), ((0, 3), 2), ((0, 1), 2), ((1, 0), 1), ((0, 1), 3),
    ((0, 3), 3), ((0, 2), 2), ((0, 2), 3), ((1, 0), 3), ((1, 1), 3), ((1, 3), 3), ((1, 2), 3),
]
X_UP_LAST = [
    ((0, 0), 0), ((0, 0), 2), ((0, 0), 1), ((0, 0), 3), ((3, 0), 0), ((0, 3), 2), ((0, 1), 2), ((0, 3), 3),
    ((0, 1), 3), ((3, 0), 2), ((0, 2), 2), ((0, 2), 3), ((3, 3), 2), ((3, 1), 2), ((3, 2), 2),
]
X_DOWN_LAST = [
    ((0, 0), 0), ((0, 0), 2), ((0, 0), 1), ((0, 0), 3), ((0, 3), 2), ((0, 1), 2), ((1, 0), 1), ((0, 3), 3),
    ((0, 1), 3), ((1, 0), 3), ((0, 2), 3), ((0, 2), 2), ((1, 3), 3), ((1, 1), 3), ((1, 2), 3),
]


def swapped(queue):
    return [((dy, dx), (chunk + 2) % 4) for (dx, dy), chunk in queue]


Z_UP = [
    (0, 0, 0), (0, 0, 1), (0, 1, 0), (0, 1, 1), (7, 0, 0), (7, 0, 1), (7, 1, 0),
    (7, 1, 1), (6, 0, 0), (6, 0, 1), (6, 1, 0), (5, 0, 0), (6, 1, 1), (5, 1, 0),
]
Z_DOWN = [((NZ - dz) % NZ, part, 1 - chunk) for dz, part, chunk in Z_UP]
Z_UP_LAST = [(dz, 0, chunk) for dz in (0, 7, 6) for chunk in range(4)] + [(5, 0, 0), (5, 0, 1)]
Z_DOWN_LAST = [
    (0, 0, 0), (0, 0, 1), (0, 0, 3), (0, 0, 2), (1, 0, 0), (1, 0, 3), (1, 0, 2),
    (1, 0, 1), (2, 0, 3), (2, 0, 2), (2, 0, 0), (2, 0, 1), (3, 0, 3), (3, 0, 2),
]
QUEUES = [
    [X_UP, X_DOWN, swapped(X_UP), swapped(X_DOWN), Z_UP, Z_DOWN],
    [X_UP_LAST, X_DOWN_LAST, swapped(X_UP_LAST), swapped(X_DOWN_LAST), Z_UP_LAST, Z_DOWN_LAST],
]

STAGES = [
    [
        (10, 0, 7, 1, 1),
        (12, 0, 11, 2, 2),
        (13, 1, 6, 2, 2),
        (15, 0, 15, 3, 2),
        (15, 0, 16, 3, 3),
        (15, 1, 8, 2, 2),
        (15, 0, 16, 4, 3),
        (15, 1, 12, 2, 2),
        (15, 0, 16, 4, 4),
        (15, 1, 14, 4, 3),
        (15, 1, 16, 4, 4),
    ],
    [
        (10, 2, 5, 1, 1),
        (12, 2, 6, 2, 1),
        (13, 2, 9, 2, 2),
        (15, 2, 11, 3, 2),
        (15, 2, 13, 3, 3),
        (15, 2, 15, 4, 3),
        (15, 2, 16, 4, 4),
    ],
]


def kernel(pattern_hbm, keep_hbm, density, out, a0, a1, wide0, slim0, b1, acc, own, pattern, keep,
           recv_a, recv_b, recv_c, send, misc):
    z = lax.axis_index("row")
    col = lax.axis_index("col")
    r = lax.axis_index("rep")
    x, y = col // NY, col % NY

    def at(dx, dy, dz):
        return ((z + dz) % NZ, ((x + dx) % NX) * NY + (y + dy) % NY, r)

    targets = [at(1, 0, 0), at(3, 0, 0), at(0, 1, 0), at(0, 3, 0), at(0, 0, 1), at(0, 0, 7)]
    other_core = (z, col, 1 - r)

    barrier = pltpu.get_barrier_semaphore()
    for target in targets + [other_core]:
        pl.semaphore_signal(barrier, inc=1, device_id=target, device_id_type=MESH)
    load = pltpu.make_async_copy(density.at[pl.ds(pl.multiple_of(r * H, H), H)], own, misc.at[0])
    load.start()
    load_pattern = pltpu.make_async_copy(pattern_hbm, pattern, misc.at[1])
    load_pattern.start()
    load_keep = pltpu.make_async_copy(keep_hbm, keep, misc.at[2])
    load_keep.start()

    meets = []
    for dz in range(NZ):
        for other in range(2):
            panel = ((z + dz) % NZ) * 2 + (1 - r if other else r)
            place = ((panel // NY + NX - x) % NX) * NY + (panel % NY + NY - y) % NY
            ranks = []
            for order in ORDERS:
                rank = jnp.int32(0)
                for j, (px, py) in enumerate(order):
                    rank = jnp.where(place == px * NY + py, j, rank)
                ranks.append(rank)
            meets.append((place, ranks))
    load_pattern.wait()
    load.wait()

    def masked_store(mask, value, store, rows, cols):
        row = rows.start
        while row < rows.stop:
            row_end = min(rows.stop, (row // BS + 1) * BS)
            for j in range(cols.start // BS, cols.stop // BS):
                kept = mask(z * 6 + r * 3 + row // BS, col * 3 + j) > 0
                here, there = slice(row, row_end), slice(j * BS, (j + 1) * BS)
                block = value(here, there)
                store(here, there, jnp.where(kept, block, jnp.zeros_like(block)).astype(jnp.bfloat16))
            row = row_end

    def store_first(rows, cols, block):
        a0[0, rows, cols] = block
        if cols.start < WIDE:
            wide0[0, r, rows, cols] = block
        else:
            slim0[0, r, rows, slice(cols.start - WIDE, cols.stop - WIDE)] = block

    def store_second(rows, cols, block):
        a1[0, rows, cols] = block
        b1[0, r, rows, cols] = block

    def remote(src, dst, send_sem, recv_sem, target):
        pltpu.make_async_remote_copy(
            src_ref=src, dst_ref=dst, send_sem=send_sem, recv_sem=recv_sem,
            device_id=target, device_id_type=MESH,
        ).start()

    def arrived(ref, sem):
        pltpu.make_async_copy(ref, ref, sem).wait()

    def there_of(direction, place):
        if direction < 4:
            shift = ((3, 0), (1, 0), (0, 3), (0, 1))[direction]
            return ((place[0] + shift[0]) % NX, (place[1] + shift[1]) % NY)
        return (place + (7, 1)[direction - 4]) % NZ

    def slot_of(place):
        return place[0] * NY + place[1]

    def chunk_rows(chunk):
        return pl.ds(FIRST_ROW[chunk], CH)

    def send_chunk(step, a, direction, place, chunk, cols):
        there = there_of(direction, place)
        remote(
            a.at[slot_of(place), chunk_rows(chunk), cols], a.at[slot_of(there), chunk_rows(chunk), cols],
            send.at[step, direction], recv_a.at[step, slot_of(there), chunk], targets[direction],
        )

    def send_piece(step, b, direction, place, part, chunk, cols=None):
        there = there_of(direction, place)
        rows = pl.ds(chunk * Z_ROWS[step], Z_ROWS[step])
        src, dst = b.at[place, r, rows], b.at[there, r, rows]
        if cols is not None:
            src, dst = b.at[place, r, rows, cols], b.at[there, r, rows, cols]
        remote(src, dst, send.at[step, direction], recv_b.at[step, there, part, chunk], targets[direction])

    def send_early(step, a):
        for chunks, directions in (((0, 2), (0, 1)), ((2, 0), (2, 3))):
            for chunk in chunks:
                for direction in directions:
                    send_chunk(step, a, direction, (0, 0), chunk, pl.ds(0, WIDE))
        for direction in (4, 5):
            if step == 0 and direction == 4:
                send_piece(step, wide0, direction, 0, 0, 0)
            elif step == 1:
                for chunk in (0, 1):
                    send_piece(step, b1, direction, 0, 0, chunk, pl.ds(0, WIDE))

    upper, lower, full = slice(0, HH), slice(HH, H), slice(0, H)
    masked = lambda rows, cols: masked_store(
        lambda i, j: pattern[i, j], lambda i, j: own[i, j], store_first, rows, cols
    )
    masked(upper, COLS[0])
    pl.semaphore_wait(barrier, 7)
    send_early(0, a0)
    masked(upper, COLS[1])
    masked(lower, full)

    for step, (a, parts) in enumerate(((a0, (wide0, slim0)), (a1, (b1,)))):
        waited = set()

        def once(*key):
            if key in waited:
                return False
            waited.add(key)
            return True

        def ensure_a(place, chunk):
            if place != (0, 0) and once("a", place, chunk):
                arrived(a.at[slot_of(place), chunk_rows(chunk)], recv_a.at[step, slot_of(place), chunk])

        def ensure_b(place, part, chunk):
            if place != 0 and once("b", place, part, chunk):
                arrived(parts[part].at[place, r, pl.ds(chunk * Z_ROWS[step], Z_ROWS[step])], recv_b.at[step, place, part, chunk])

        def ensure_c(place, part):
            if once("c", place, part):
                arrived(parts[part].at[place, 1 - r], recv_c.at[step, place, part])

        def share(place, part):
            if once("s", place, part):
                ref = parts[part].at[place, r]
                remote(ref, ref, send.at[step, 6], recv_c.at[step, place, part], other_core)

        def issue(k):
            for direction, queue in enumerate(QUEUES[step]):
                if k >= len(queue):
                    continue
                rest = pl.ds(WIDE, H - WIDE)
                if direction < 4:
                    place, chunk = queue[k]
                    ensure_a(place, chunk)
                    early = place == (0, 0) and chunk in (0, 2)
                    send_chunk(step, a, direction, place, chunk, rest if early else pl.ds(0, H))
                else:
                    place, part, chunk = queue[k]
                    ensure_b(place, part, chunk)
                    if step == 1:
                        send_piece(step, b1, direction, place, 0, chunk, rest if place == 0 and chunk < 2 else None)
                    elif (direction, place, part, chunk) != (4, 0, 0, 0):
                        send_piece(step, parts[part], direction, place, part, chunk)
            for place in range(1, NZ):
                for part in range(len(parts)):
                    if all(("b", place, part, chunk) in waited for chunk in range(H // Z_ROWS[step])):
                        share(place, part)

        def products(region, count, mine, shared, before):
            count0, mine0, shared0 = before
            order = ORDERS[region]
            items = []
            for i in range(count0, count):
                dx, dy = order[i]
                panel = ((x + dx) % NX) * NY + (y + dy) % NY
                rp = panel % 2
                dz = (panel // 2 + NZ - z) % NZ
                far = jnp.where(dz > 4, NZ - dz, dz)
                reach = jnp.where(rp == r, mine, shared)
                items.append((jnp.int32(slot_of((dx, dy))), dz, rp, jnp.where(far <= reach, 1, 0)))
            for reach0, reach, other in ((mine0, mine, 0), (shared0, shared, 1)):
                for near in range(reach0 + 1, reach + 1):
                    for dz in sorted({near, (NZ - near) % NZ}):
                        place, ranks = meets[dz * 2 + other]
                        rp = 1 - r if other else r
                        items.append((place, jnp.int32(dz), rp, jnp.where(ranks[region] < count0, 1, 0)))

            if not items:
                return
            total, picks = jnp.int32(0), []
            for slot, dz, rp, ready in items:
                picks.append((jnp.where(ready > 0, total, -1), slot * 16 + dz * 2 + rp))
                total = total + ready

            def add(first, size):
                slots, halves = [], []
                for n in range(size):
                    code = jnp.int32(0)
                    for rank, item in picks:
                        code = jnp.where(rank == first + n, item, code)
                    slots.append(lax.div(code, 16))
                    halves.append((lax.rem(lax.div(code, 2), NZ), lax.rem(code, 2)))
                if region == 0:
                    terms = [(upper, COLS[0], wide0)]
                elif region == 1:
                    terms = [(lower, COLS[0], wide0), (full, COLS[1], slim0)]
                else:
                    terms = [(full, full, b1)]
                for rows, cols, b in terms:
                    left = jnp.concatenate([a[slot, rows] for slot in slots], axis=1)
                    right = jnp.concatenate([b[dz, rp] for dz, rp in halves], axis=0)
                    acc[rows, cols] += jnp.dot(left, right, preferred_element_type=jnp.float32)

            size = GROUP
            while size > len(items):
                size //= 2

            @pl.loop(0, total // size)
            def _(j):
                add(j * size, size)

            while size > 1:
                size //= 2

                @pl.when(total // size % 2 == 1)
                def _():
                    add(total // (2 * size) * (2 * size), size)

        issue(0)
        issue(1)
        for part in range(len(parts)):
            share(0, part)
        issue(2)
        acc[...] = jnp.zeros_like(acc)

        before = [(0, -1, -1)] * 3
        stages = list(STAGES[step])
        for k in range(3, 15):
            issue(k)
            while stages and stages[0][0] == k + 1:
                _, region, count, mine, shared = stages.pop(0)
                needed = range(1 if region == 0 else len(parts))
                for place in ORDERS[region][:count]:
                    for chunk in (0, 2) if region == 0 else (0, 1, 2, 3):
                        ensure_a(place, chunk)
                for near in range(0, mine + 1):
                    for dz in sorted({near, (NZ - near) % NZ}):
                        for part in needed:
                            for chunk in range(H // Z_ROWS[step]):
                                ensure_b(dz, part, chunk)
                            share(dz, part)
                for near in range(0, shared + 1):
                    for dz in sorted({near, (NZ - near) % NZ}):
                        for part in needed:
                            ensure_c(dz, part)
                if not stages:
                    for direction, queue in enumerate(QUEUES[step]):
                        arrived(a.at[pl.ds(0, len(queue)), pl.ds(0, CH)], send.at[step, direction])
                    arrived(a.at[pl.ds(0, NZ)], send.at[step, 6])
                products(region, count, mine, shared, before[region])
                before[region] = (count, mine, shared)
                if step == 0 and region == 0 and (count, mine, shared) == (16, 4, 4):
                    masked = lambda rows, cols: masked_store(
                        lambda i, j: keep[0, i, j], lambda i, j: acc[i, j], store_second, rows, cols
                    )
                    load_keep.wait()
                    masked(upper, COLS[0])
                    send_early(1, a1)

        if step == 0:
            masked(upper, COLS[1])
            masked(lower, full)

    copies = []
    for i in range(3):
        rows = slice(i * BS, (i + 1) * BS)
        there = pl.ds(pl.multiple_of(r * H + i * BS, BS), BS)
        for j in range(3):
            cols = slice(j * BS, (j + 1) * BS)
            block = 2.0 * a1[0, rows, cols].astype(jnp.float32) - acc[rows, cols]
            kept = keep[1, z * 6 + r * 3 + i, col * 3 + j] > 0
            out[there, cols] = jnp.where(kept, block, jnp.zeros_like(block)).astype(jnp.bfloat16)
        copy = pltpu.make_async_remote_copy(
            src_ref=out.at[there], dst_ref=out.at[there], send_sem=misc.at[3 + i], recv_sem=misc.at[6 + i],
            device_id=other_core, device_id_type=MESH,
        )
        copy.start()
        copies.append(copy)
    for copy in copies:
        copy.wait()


def shards(density, pattern, keep):
    hbm = pl.BlockSpec(memory_space=pl.ANY)
    bf16 = jnp.bfloat16
    return pl.pallas_call(
        kernel,
        out_shape=pltpu.VMEM(density.shape, bf16),
        in_specs=[hbm, hbm, hbm],
        out_specs=pl.BlockSpec(memory_space=pltpu.VMEM),
        scratch_shapes=[
            pltpu.VMEM((NX * NY, H, H), bf16),
            pltpu.VMEM((NX * NY, H, H), bf16),
            pltpu.VMEM((NZ, 2, H, WIDE), bf16),
            pltpu.VMEM((NZ, 2, H, H - WIDE), bf16),
            pltpu.VMEM((NZ, 2, H, H), bf16),
            pltpu.VMEM((H, H), jnp.float32),
            pltpu.VMEM((H, H), bf16),
            pltpu.SMEM(pattern.shape, jnp.int32),
            pltpu.SMEM(keep.shape, jnp.int32),
            pltpu.SemaphoreType.DMA((2, NX * NY, 4)),
            pltpu.SemaphoreType.DMA((2, NZ, 2, 4)),
            pltpu.SemaphoreType.DMA((2, NZ, 2)),
            pltpu.SemaphoreType.DMA((2, 7)),
            pltpu.SemaphoreType.DMA((9,)),
        ],
        name="purify",
        cost_estimate=pl.CostEstimate(flops=2 * 2 * H * H * 6144, bytes_accessed=2 * 768 * H * 2, transcendentals=0),
        compiler_params=pltpu.CompilerParams(
            collective_id=0, has_side_effects=True, vmem_limit_bytes=60 * 2**20
        ),
    )(pattern, keep, density)


def solution(mesh):
    in_specs = (P("row", "col"), P(), P())
    out_specs = P("row", "col")
    return jax.shard_map(shards, mesh=mesh, in_specs=in_specs, out_specs=out_specs, check_vma=False)
```

```python
import jax
import jax.numpy as jnp
from jax import lax
from jax.experimental import pallas as pl
from jax.experimental.pallas import tpu as pltpu
from jax.sharding import PartitionSpec as P

BS = 128
NX, NY, NZ = 4, 4, 8
H = 384
CH = 96
HH = 192
Z_ROWS = (HH, CH)
WIDE = 256
FIRST_ROW = (0, 192, 96, 288)
COLS = (slice(0, WIDE), slice(WIDE, H))
GROUP = 4
MESH = pl.DeviceIdType.MESH

ORDER_UPPER = [
    (0, 0), (1, 0), (3, 0), (0, 1), (0, 3), (3, 3), (1, 1), (3, 1),
    (1, 3), (2, 0), (0, 2), (3, 2), (2, 3), (2, 1), (1, 2), (2, 2),
]
ORDER_REST = [
    (0, 0), (1, 0), (3, 0), (0, 1), (0, 3), (1, 1), (2, 0), (0, 2),
    (2, 1), (1, 2), (3, 1), (1, 3), (2, 3), (3, 2), (2, 2), (3, 3),
]
ORDER_LAST = [
    (0, 0), (1, 0), (3, 0), (0, 1), (0, 3), (3, 3), (1, 3), (1, 1),
    (3, 1), (2, 0), (0, 2), (2, 3), (3, 2), (2, 1), (1, 2), (2, 2),
]
ORDERS = [ORDER_UPPER, ORDER_REST, ORDER_LAST]

X_UP = [
    ((0, 0), 0), ((0, 0), 2), ((0, 0), 1), ((0, 0), 3), ((3, 0), 0), ((0, 3), 2), ((0, 1), 2), ((3, 0), 2),
    ((0, 2), 2), ((3, 3), 2), ((3, 1), 2), ((3, 2), 2), ((0, 1), 3), ((0, 2), 3), ((0, 3), 3),
]
X_DOWN = [
    ((0, 0), 0), ((0, 0), 2), ((0, 0), 1), ((0, 0), 3), ((0, 3), 2), ((0, 1), 2), ((1, 0), 1), ((0, 1), 3),
    ((0, 3), 3), ((0, 2), 2), ((0, 2), 3), ((1, 0), 3), ((1, 1), 3), ((1, 3), 3), ((1, 2), 3),
]
X_UP_LAST = [
    ((0, 0), 0), ((0, 0), 2), ((0, 0), 1), ((0, 0), 3), ((3, 0), 0), ((0, 3), 2), ((0, 1), 2), ((0, 3), 3),
    ((0, 1), 3), ((3, 0), 2), ((0, 2), 2), ((0, 2), 3), ((3, 3), 2), ((3, 1), 2), ((3, 2), 2),
]
X_DOWN_LAST = [
    ((0, 0), 0), ((0, 0), 2), ((0, 0), 1), ((0, 0), 3), ((0, 3), 2), ((0, 1), 2), ((1, 0), 1), ((0, 3), 3),
    ((0, 1), 3), ((1, 0), 3), ((0, 2), 3), ((0, 2), 2), ((1, 3), 3), ((1, 1), 3), ((1, 2), 3),
]


def swapped(queue):
    return [((dy, dx), (chunk + 2) % 4) for (dx, dy), chunk in queue]


Z_UP = [
    (0, 0, 0), (0, 0, 1), (0, 1, 0), (0, 1, 1), (7, 0, 0), (7, 0, 1), (7, 1, 0),
    (7, 1, 1), (6, 0, 0), (6, 0, 1), (6, 1, 0), (5, 0, 0), (6, 1, 1), (5, 1, 0),
]
Z_DOWN = [((NZ - dz) % NZ, part, 1 - chunk) for dz, part, chunk in Z_UP]
Z_UP_LAST = [(dz, 0, chunk) for dz in (0, 7, 6) for chunk in range(4)] + [(5, 0, 0), (5, 0, 1)]
Z_DOWN_LAST = [
    (0, 0, 0), (0, 0, 1), (0, 0, 3), (0, 0, 2), (1, 0, 0), (1, 0, 3), (1, 0, 2),
    (1, 0, 1), (2, 0, 3), (2, 0, 2), (2, 0, 0), (2, 0, 1), (3, 0, 3), (3, 0, 2),
]
QUEUES = [
    [X_UP, X_DOWN, swapped(X_UP), swapped(X_DOWN), Z_UP, Z_DOWN],
    [X_UP_LAST, X_DOWN_LAST, swapped(X_UP_LAST), swapped(X_DOWN_LAST), Z_UP_LAST, Z_DOWN_LAST],
]

STAGES = [
    [
        (10, 0, 7, 1, 1),
        (12, 0, 11, 2, 2),
        (13, 1, 6, 2, 2),
        (15, 0, 15, 3, 2),
        (15, 0, 16, 3, 3),
        (15, 1, 8, 2, 2),
        (15, 0, 16, 4, 3),
        (15, 0, 16, 4, 4),
        (15, 1, 12, 3, 2),
        (15, 1, 14, 4, 3),
        (15, 1, 16, 4, 4),
    ],
    [
        (10, 2, 5, 1, 1),
        (12, 2, 6, 2, 1),
        (13, 2, 9, 2, 2),
        (15, 2, 11, 3, 2),
        (15, 2, 13, 3, 3),
        (15, 2, 15, 4, 3),
        (15, 2, 16, 4, 4),
    ],
]


def kernel(pattern_hbm, keep_hbm, density, out, a0, a1, wide0, slim0, b1, acc, own, pattern, keep,
           recv_a, recv_b, recv_c, send, misc):
    z = lax.axis_index("row")
    col = lax.axis_index("col")
    r = lax.axis_index("rep")
    x, y = col // NY, col % NY

    def at(dx, dy, dz):
        return ((z + dz) % NZ, ((x + dx) % NX) * NY + (y + dy) % NY, r)

    targets = [at(1, 0, 0), at(3, 0, 0), at(0, 1, 0), at(0, 3, 0), at(0, 0, 1), at(0, 0, 7)]
    other_core = (z, col, 1 - r)

    barrier = pltpu.get_barrier_semaphore()
    for target in targets + [other_core]:
        pl.semaphore_signal(barrier, inc=1, device_id=target, device_id_type=MESH)
    load = pltpu.make_async_copy(density.at[pl.ds(pl.multiple_of(r * H, H), H)], own, misc.at[0])
    load.start()
    load_pattern = pltpu.make_async_copy(pattern_hbm, pattern, misc.at[1])
    load_pattern.start()
    load_keep = pltpu.make_async_copy(keep_hbm, keep, misc.at[2])
    load_keep.start()

    meets = []
    for dz in range(NZ):
        for other in range(2):
            panel = ((z + dz) % NZ) * 2 + (1 - r if other else r)
            place = ((panel // NY + NX - x) % NX) * NY + (panel % NY + NY - y) % NY
            ranks = []
            for order in ORDERS:
                rank = jnp.int32(0)
                for j, (px, py) in enumerate(order):
                    rank = jnp.where(place == px * NY + py, j, rank)
                ranks.append(rank)
            meets.append((place, ranks))
    load_pattern.wait()
    load.wait()

    def masked_store(mask, value, store, rows, cols):
        row = rows.start
        while row < rows.stop:
            row_end = min(rows.stop, (row // BS + 1) * BS)
            for j in range(cols.start // BS, cols.stop // BS):
                kept = mask(z * 6 + r * 3 + row // BS, col * 3 + j) > 0
                here, there = slice(row, row_end), slice(j * BS, (j + 1) * BS)
                block = value(here, there)
                store(here, there, jnp.where(kept, block, jnp.zeros_like(block)).astype(jnp.bfloat16))
            row = row_end

    def store_first(rows, cols, block):
        a0[0, rows, cols] = block
        if cols.start < WIDE:
            wide0[0, r, rows, cols] = block
        else:
            slim0[0, r, rows, slice(cols.start - WIDE, cols.stop - WIDE)] = block

    def store_second(rows, cols, block):
        a1[0, rows, cols] = block
        b1[0, r, rows, cols] = block

    def remote(src, dst, send_sem, recv_sem, target):
        pltpu.make_async_remote_copy(
            src_ref=src, dst_ref=dst, send_sem=send_sem, recv_sem=recv_sem,
            device_id=target, device_id_type=MESH,
        ).start()

    def arrived(ref, sem):
        pltpu.make_async_copy(ref, ref, sem).wait()

    def there_of(direction, place):
        if direction < 4:
            shift = ((3, 0), (1, 0), (0, 3), (0, 1))[direction]
            return ((place[0] + shift[0]) % NX, (place[1] + shift[1]) % NY)
        return (place + (7, 1)[direction - 4]) % NZ

    def slot_of(place):
        return place[0] * NY + place[1]

    def chunk_rows(chunk):
        return pl.ds(FIRST_ROW[chunk], CH)

    def send_chunk(step, a, direction, place, chunk, cols):
        there = there_of(direction, place)
        remote(
            a.at[slot_of(place), chunk_rows(chunk), cols], a.at[slot_of(there), chunk_rows(chunk), cols],
            send.at[step, direction], recv_a.at[step, slot_of(there), chunk], targets[direction],
        )

    def send_piece(step, b, direction, place, part, chunk, cols=None):
        there = there_of(direction, place)
        rows = pl.ds(chunk * Z_ROWS[step], Z_ROWS[step])
        src, dst = b.at[place, r, rows], b.at[there, r, rows]
        if cols is not None:
            src, dst = b.at[place, r, rows, cols], b.at[there, r, rows, cols]
        remote(src, dst, send.at[step, direction], recv_b.at[step, there, part, chunk], targets[direction])

    def send_early(step, a):
        for chunks, directions in (((0, 2), (0, 1)), ((2, 0), (2, 3))):
            for chunk in chunks:
                for direction in directions:
                    send_chunk(step, a, direction, (0, 0), chunk, pl.ds(0, WIDE))
        for direction in (4, 5):
            if step == 0 and direction == 4:
                send_piece(step, wide0, direction, 0, 0, 0)
            elif step == 1:
                for chunk in (0, 1):
                    send_piece(step, b1, direction, 0, 0, chunk, pl.ds(0, WIDE))

    upper, lower, full = slice(0, HH), slice(HH, H), slice(0, H)
    masked = lambda rows, cols: masked_store(
        lambda i, j: pattern[i, j], lambda i, j: own[i, j], store_first, rows, cols
    )
    masked(upper, COLS[0])
    pl.semaphore_wait(barrier, 7)
    send_early(0, a0)
    masked(upper, COLS[1])
    masked(lower, full)

    for step, (a, parts) in enumerate(((a0, (wide0, slim0)), (a1, (b1,)))):
        waited = set()

        def once(*key):
            if key in waited:
                return False
            waited.add(key)
            return True

        def ensure_a(place, chunk):
            if place != (0, 0) and once("a", place, chunk):
                arrived(a.at[slot_of(place), chunk_rows(chunk)], recv_a.at[step, slot_of(place), chunk])

        def ensure_b(place, part, chunk):
            if place != 0 and once("b", place, part, chunk):
                ref = parts[part].at[place, r, pl.ds(chunk * Z_ROWS[step], Z_ROWS[step])]
                arrived(ref, recv_b.at[step, place, part, chunk])
                remote(ref, ref, send.at[step, 6], recv_c.at[step, place, part], other_core)

        def ensure_c(place, part):
            if once("c", place, part):
                arrived(parts[part].at[place, 1 - r], recv_c.at[step, place, part])

        def share(place, part):
            if once("s", place, part):
                ref = parts[part].at[place, r]
                remote(ref, ref, send.at[step, 6], recv_c.at[step, place, part], other_core)

        def issue(k):
            for direction, queue in enumerate(QUEUES[step]):
                if k >= len(queue):
                    continue
                rest = pl.ds(WIDE, H - WIDE)
                if direction < 4:
                    place, chunk = queue[k]
                    ensure_a(place, chunk)
                    early = place == (0, 0) and chunk in (0, 2)
                    send_chunk(step, a, direction, place, chunk, rest if early else pl.ds(0, H))
                else:
                    place, part, chunk = queue[k]
                    ensure_b(place, part, chunk)
                    if step == 1:
                        send_piece(step, b1, direction, place, 0, chunk, rest if place == 0 and chunk < 2 else None)
                    elif (direction, place, part, chunk) != (4, 0, 0, 0):
                        send_piece(step, parts[part], direction, place, part, chunk)

        def products(region, count, mine, shared, before):
            count0, mine0, shared0 = before
            order = ORDERS[region]
            items = []
            for i in range(count0, count):
                dx, dy = order[i]
                panel = ((x + dx) % NX) * NY + (y + dy) % NY
                rp = panel % 2
                dz = (panel // 2 + NZ - z) % NZ
                far = jnp.where(dz > 4, NZ - dz, dz)
                reach = jnp.where(rp == r, mine, shared)
                items.append((jnp.int32(slot_of((dx, dy))), dz, rp, jnp.where(far <= reach, 1, 0)))
            for reach0, reach, other in ((mine0, mine, 0), (shared0, shared, 1)):
                for near in range(reach0 + 1, reach + 1):
                    for dz in sorted({near, (NZ - near) % NZ}):
                        place, ranks = meets[dz * 2 + other]
                        rp = 1 - r if other else r
                        items.append((place, jnp.int32(dz), rp, jnp.where(ranks[region] < count0, 1, 0)))

            if not items:
                return
            total, picks = jnp.int32(0), []
            for slot, dz, rp, ready in items:
                picks.append((jnp.where(ready > 0, total, -1), slot * 16 + dz * 2 + rp))
                total = total + ready

            def add(first, size):
                slots, halves = [], []
                for n in range(size):
                    code = jnp.int32(0)
                    for rank, item in picks:
                        code = jnp.where(rank == first + n, item, code)
                    slots.append(lax.div(code, 16))
                    halves.append((lax.rem(lax.div(code, 2), NZ), lax.rem(code, 2)))
                if region == 0:
                    terms = [(upper, COLS[0], wide0)]
                elif region == 1:
                    terms = [(lower, COLS[0], wide0), (full, COLS[1], slim0)]
                else:
                    terms = [(full, full, b1)]
                for rows, cols, b in terms:
                    left = jnp.concatenate([a[slot, rows] for slot in slots], axis=1)
                    right = jnp.concatenate([b[dz, rp] for dz, rp in halves], axis=0)
                    acc[rows, cols] += jnp.dot(left, right, preferred_element_type=jnp.float32)

            size = GROUP
            while size > len(items):
                size //= 2

            @pl.loop(0, total // size)
            def _(j):
                add(j * size, size)

            while size > 1:
                size //= 2

                @pl.when(total // size % 2 == 1)
                def _():
                    add(total // (2 * size) * (2 * size), size)

        issue(0)
        issue(1)
        for part in range(len(parts)):
            share(0, part)
        issue(2)
        acc[...] = jnp.zeros_like(acc)

        before = [(0, -1, -1)] * 3
        stages = list(STAGES[step])
        for k in range(3, 15):
            issue(k)
            while stages and stages[0][0] == k + 1:
                _, region, count, mine, shared = stages.pop(0)
                needed = range(1 if region == 0 else len(parts))
                for place in ORDERS[region][:count]:
                    for chunk in (0, 2) if region == 0 else (0, 1, 2, 3):
                        ensure_a(place, chunk)
                for near in range(0, mine + 1):
                    for dz in sorted({near, (NZ - near) % NZ}):
                        for part in needed:
                            for chunk in range(H // Z_ROWS[step]):
                                ensure_b(dz, part, chunk)
                for near in range(0, shared + 1):
                    for dz in sorted({near, (NZ - near) % NZ}):
                        for part in needed:
                            ensure_c(dz, part)
                if not stages:
                    for direction, queue in enumerate(QUEUES[step]):
                        arrived(a.at[pl.ds(0, len(queue)), pl.ds(0, CH)], send.at[step, direction])
                    arrived(a.at[pl.ds(0, NZ)], send.at[step, 6])
                products(region, count, mine, shared, before[region])
                before[region] = (count, mine, shared)
                if step == 0 and region == 0 and (count, mine, shared) == (16, 4, 4):
                    masked = lambda rows, cols: masked_store(
                        lambda i, j: keep[0, i, j], lambda i, j: acc[i, j], store_second, rows, cols
                    )
                    load_keep.wait()
                    masked(upper, COLS[0])
                    send_early(1, a1)

        if step == 0:
            masked(upper, COLS[1])
            masked(lower, full)

    copies = []
    for i in range(3):
        rows = slice(i * BS, (i + 1) * BS)
        there = pl.ds(pl.multiple_of(r * H + i * BS, BS), BS)
        for j in range(3):
            cols = slice(j * BS, (j + 1) * BS)
            block = 2.0 * a1[0, rows, cols].astype(jnp.float32) - acc[rows, cols]
            kept = keep[1, z * 6 + r * 3 + i, col * 3 + j] > 0
            out[there, cols] = jnp.where(kept, block, jnp.zeros_like(block)).astype(jnp.bfloat16)
        copy = pltpu.make_async_remote_copy(
            src_ref=out.at[there], dst_ref=out.at[there], send_sem=misc.at[3 + i], recv_sem=misc.at[6 + i],
            device_id=other_core, device_id_type=MESH,
        )
        copy.start()
        copies.append(copy)
    for copy in copies:
        copy.wait()


def shards(density, pattern, keep):
    hbm = pl.BlockSpec(memory_space=pl.ANY)
    bf16 = jnp.bfloat16
    return pl.pallas_call(
        kernel,
        out_shape=pltpu.VMEM(density.shape, bf16),
        in_specs=[hbm, hbm, hbm],
        out_specs=pl.BlockSpec(memory_space=pltpu.VMEM),
        scratch_shapes=[
            pltpu.VMEM((NX * NY, H, H), bf16),
            pltpu.VMEM((NX * NY, H, H), bf16),
            pltpu.VMEM((NZ, 2, H, WIDE), bf16),
            pltpu.VMEM((NZ, 2, H, H - WIDE), bf16),
            pltpu.VMEM((NZ, 2, H, H), bf16),
            pltpu.VMEM((H, H), jnp.float32),
            pltpu.VMEM((H, H), bf16),
            pltpu.SMEM(pattern.shape, jnp.int32),
            pltpu.SMEM(keep.shape, jnp.int32),
            pltpu.SemaphoreType.DMA((2, NX * NY, 4)),
            pltpu.SemaphoreType.DMA((2, NZ, 2, 4)),
            pltpu.SemaphoreType.DMA((2, NZ, 2)),
            pltpu.SemaphoreType.DMA((2, 7)),
            pltpu.SemaphoreType.DMA((9,)),
        ],
        name="purify",
        cost_estimate=pl.CostEstimate(flops=2 * 2 * H * H * 6144, bytes_accessed=2 * 768 * H * 2, transcendentals=0),
        compiler_params=pltpu.CompilerParams(
            collective_id=0, has_side_effects=True, vmem_limit_bytes=60 * 2**20
        ),
    )(pattern, keep, density)


def solution(mesh):
    in_specs = (P("row", "col"), P(), P())
    out_specs = P("row", "col")
    return jax.shard_map(shards, mesh=mesh, in_specs=in_specs, out_specs=out_specs, check_vma=False)
```

```python
import jax
import jax.numpy as jnp
from jax import lax
from jax.experimental import pallas as pl
from jax.experimental.pallas import tpu as pltpu
from jax.sharding import PartitionSpec as P

BS = 128
NX, NY, NZ = 4, 4, 8
H = 384
CH = 96
HH = 192
Z_ROWS = (HH, CH)
WIDE = 256
FIRST_ROW = (0, 192, 96, 288)
COLS = (slice(0, WIDE), slice(WIDE, H))
GROUP = 4
MESH = pl.DeviceIdType.MESH

ORDER_UPPER = [
    (0, 0), (1, 0), (3, 0), (0, 1), (0, 3), (3, 3), (1, 1), (3, 1),
    (1, 3), (2, 0), (0, 2), (3, 2), (2, 3), (2, 1), (1, 2), (2, 2),
]
ORDER_REST = [
    (0, 0), (1, 0), (3, 0), (0, 1), (0, 3), (1, 1), (2, 0), (0, 2),
    (2, 1), (1, 2), (3, 1), (1, 3), (2, 3), (3, 2), (2, 2), (3, 3),
]
ORDER_LAST = [
    (0, 0), (1, 0), (3, 0), (0, 1), (0, 3), (3, 3), (1, 3), (1, 1),
    (3, 1), (2, 0), (0, 2), (2, 3), (3, 2), (2, 1), (1, 2), (2, 2),
]
ORDERS = [ORDER_UPPER, ORDER_REST, ORDER_LAST]

X_UP = [
    ((0, 0), 0), ((0, 0), 2), ((0, 0), 1), ((0, 0), 3), ((3, 0), 0), ((0, 3), 2), ((0, 1), 2), ((3, 0), 2),
    ((0, 2), 2), ((3, 3), 2), ((3, 1), 2), ((3, 2), 2), ((0, 1), 3), ((0, 2), 3), ((0, 3), 3),
]
X_DOWN = [
    ((0, 0), 0), ((0, 0), 2), ((0, 0), 1), ((0, 0), 3), ((0, 3), 2), ((0, 1), 2), ((1, 0), 1), ((0, 1), 3),
    ((0, 3), 3), ((0, 2), 2), ((0, 2), 3), ((1, 0), 3), ((1, 1), 3), ((1, 3), 3), ((1, 2), 3),
]
X_UP_LAST = [
    ((0, 0), 0), ((0, 0), 2), ((0, 0), 1), ((0, 0), 3), ((3, 0), 0), ((0, 3), 2), ((0, 1), 2), ((0, 3), 3),
    ((0, 1), 3), ((3, 0), 2), ((0, 2), 2), ((0, 2), 3), ((3, 3), 2), ((3, 1), 2), ((3, 2), 2),
]
X_DOWN_LAST = [
    ((0, 0), 0), ((0, 0), 2), ((0, 0), 1), ((0, 0), 3), ((0, 3), 2), ((0, 1), 2), ((1, 0), 1), ((0, 3), 3),
    ((0, 1), 3), ((1, 0), 3), ((0, 2), 3), ((0, 2), 2), ((1, 3), 3), ((1, 1), 3), ((1, 2), 3),
]


def swapped(queue):
    return [((dy, dx), (chunk + 2) % 4) for (dx, dy), chunk in queue]


Z_UP = [
    (0, 0, 0), (0, 0, 1), (0, 1, 0), (0, 1, 1), (7, 0, 0), (7, 0, 1), (7, 1, 0),
    (7, 1, 1), (6, 0, 0), (6, 0, 1), (6, 1, 0), (5, 0, 0), (6, 1, 1), (5, 1, 0),
]
Z_DOWN = [((NZ - dz) % NZ, part, 1 - chunk) for dz, part, chunk in Z_UP]
Z_UP_LAST = [(dz, 0, chunk) for dz in (0, 7, 6) for chunk in range(4)] + [(5, 0, 0), (5, 0, 1)]
Z_DOWN_LAST = [
    (0, 0, 0), (0, 0, 1), (0, 0, 3), (0, 0, 2), (1, 0, 0), (1, 0, 3), (1, 0, 2),
    (1, 0, 1), (2, 0, 3), (2, 0, 2), (2, 0, 0), (2, 0, 1), (3, 0, 3), (3, 0, 2),
]
QUEUES = [
    [X_UP, X_DOWN, swapped(X_UP), swapped(X_DOWN), Z_UP, Z_DOWN],
    [X_UP_LAST, X_DOWN_LAST, swapped(X_UP_LAST), swapped(X_DOWN_LAST), Z_UP_LAST, Z_DOWN_LAST],
]

STAGES = [
    [
        (10, 0, 7, 1, 1),
        (12, 0, 11, 2, 2),
        (13, 1, 6, 2, 2),
        (15, 0, 15, 3, 2),
        (15, 0, 16, 3, 3),
        (15, 1, 8, 2, 2),
        (15, 0, 16, 4, 3),
        (15, 0, 16, 4, 4),
        (15, 1, 12, 3, 2),
        (15, 1, 14, 4, 3),
        (15, 1, 16, 4, 4),
    ],
    [
        (10, 2, 5, 1, 1),
        (12, 2, 6, 2, 1),
        (13, 2, 9, 2, 2),
        (15, 2, 11, 3, 2),
        (15, 2, 13, 3, 3),
        (15, 2, 15, 4, 3),
        (15, 2, 16, 4, 4),
    ],
]


def kernel(pattern_hbm, keep_hbm, density, out, a0, a1, wide0, slim0, b1, acc, own, pattern, keep,
           recv_a, recv_b, recv_c, send, misc):
    z = lax.axis_index("row")
    col = lax.axis_index("col")
    r = lax.axis_index("rep")
    x, y = col // NY, col % NY

    def at(dx, dy, dz):
        return ((z + dz) % NZ, ((x + dx) % NX) * NY + (y + dy) % NY, r)

    targets = [at(1, 0, 0), at(3, 0, 0), at(0, 1, 0), at(0, 3, 0), at(0, 0, 1), at(0, 0, 7)]
    other_core = (z, col, 1 - r)

    barrier = pltpu.get_barrier_semaphore()
    for target in targets + [other_core]:
        pl.semaphore_signal(barrier, inc=1, device_id=target, device_id_type=MESH)
    load = pltpu.make_async_copy(density.at[pl.ds(pl.multiple_of(r * H, H), H)], own, misc.at[0])
    load.start()
    load_pattern = pltpu.make_async_copy(pattern_hbm, pattern, misc.at[1])
    load_pattern.start()
    load_keep = pltpu.make_async_copy(keep_hbm, keep, misc.at[2])
    load_keep.start()

    meets = []
    for dz in range(NZ):
        for other in range(2):
            panel = ((z + dz) % NZ) * 2 + (1 - r if other else r)
            place = ((panel // NY + NX - x) % NX) * NY + (panel % NY + NY - y) % NY
            ranks = []
            for order in ORDERS:
                rank = jnp.int32(0)
                for j, (px, py) in enumerate(order):
                    rank = jnp.where(place == px * NY + py, j, rank)
                ranks.append(rank)
            meets.append((place, ranks))
    load_pattern.wait()
    load.wait()

    def masked_store(mask, value, store, rows, cols):
        row = rows.start
        while row < rows.stop:
            row_end = min(rows.stop, (row // BS + 1) * BS)
            for j in range(cols.start // BS, cols.stop // BS):
                kept = mask(z * 6 + r * 3 + row // BS, col * 3 + j) > 0
                here, there = slice(row, row_end), slice(j * BS, (j + 1) * BS)
                block = value(here, there)
                store(here, there, jnp.where(kept, block, jnp.zeros_like(block)).astype(jnp.bfloat16))
            row = row_end

    def store_first(rows, cols, block):
        a0[0, rows, cols] = block
        if cols.start < WIDE:
            wide0[0, r, rows, cols] = block
        else:
            slim0[0, r, rows, slice(cols.start - WIDE, cols.stop - WIDE)] = block

    def store_second(rows, cols, block):
        a1[0, rows, cols] = block
        b1[0, r, rows, cols] = block

    def remote(src, dst, send_sem, recv_sem, target):
        pltpu.make_async_remote_copy(
            src_ref=src, dst_ref=dst, send_sem=send_sem, recv_sem=recv_sem,
            device_id=target, device_id_type=MESH,
        ).start()

    def arrived(ref, sem):
        pltpu.make_async_copy(ref, ref, sem).wait()

    def there_of(direction, place):
        if direction < 4:
            shift = ((3, 0), (1, 0), (0, 3), (0, 1))[direction]
            return ((place[0] + shift[0]) % NX, (place[1] + shift[1]) % NY)
        return (place + (7, 1)[direction - 4]) % NZ

    def slot_of(place):
        return place[0] * NY + place[1]

    def chunk_rows(chunk):
        return pl.ds(FIRST_ROW[chunk], CH)

    def send_chunk(step, a, direction, place, chunk, cols):
        there = there_of(direction, place)
        remote(
            a.at[slot_of(place), chunk_rows(chunk), cols], a.at[slot_of(there), chunk_rows(chunk), cols],
            send.at[step, direction], recv_a.at[step, slot_of(there), chunk], targets[direction],
        )

    def send_piece(step, b, direction, place, part, chunk, cols=None):
        there = there_of(direction, place)
        rows = pl.ds(chunk * Z_ROWS[step], Z_ROWS[step])
        src, dst = b.at[place, r, rows], b.at[there, r, rows]
        if cols is not None:
            src, dst = b.at[place, r, rows, cols], b.at[there, r, rows, cols]
        remote(src, dst, send.at[step, direction], recv_b.at[step, there, part, chunk], targets[direction])

    def send_early(step, a):
        for chunks, directions in (((0, 2), (0, 1)), ((2, 0), (2, 3))):
            for chunk in chunks:
                for direction in directions:
                    send_chunk(step, a, direction, (0, 0), chunk, pl.ds(0, WIDE))
        for direction in (4, 5):
            if step == 0 and direction == 4:
                send_piece(step, wide0, direction, 0, 0, 0)
            elif step == 1:
                for chunk in (0, 1):
                    send_piece(step, b1, direction, 0, 0, chunk, pl.ds(0, WIDE))

    upper, lower, full = slice(0, HH), slice(HH, H), slice(0, H)
    masked = lambda rows, cols: masked_store(
        lambda i, j: pattern[i, j], lambda i, j: own[i, j], store_first, rows, cols
    )
    masked(upper, COLS[0])
    pl.semaphore_wait(barrier, 7)
    send_early(0, a0)
    masked(upper, COLS[1])
    masked(lower, full)

    for step, (a, parts) in enumerate(((a0, (wide0, slim0)), (a1, (b1,)))):
        waited = set()

        def once(*key):
            if key in waited:
                return False
            waited.add(key)
            return True

        def ensure_a(place, chunk):
            if place != (0, 0) and once("a", place, chunk):
                arrived(a.at[slot_of(place), chunk_rows(chunk)], recv_a.at[step, slot_of(place), chunk])

        def ensure_b(place, part, chunk):
            if place != 0 and once("b", place, part, chunk):
                ref = parts[part].at[place, r, pl.ds(chunk * Z_ROWS[step], Z_ROWS[step])]
                arrived(ref, recv_b.at[step, place, part, chunk])
                remote(ref, ref, send.at[step, 6], recv_c.at[step, place, part], other_core)

        def ensure_c(place, part):
            if once("c", place, part):
                arrived(parts[part].at[place, 1 - r], recv_c.at[step, place, part])

        def share(place, part):
            if once("s", place, part):
                ref = parts[part].at[place, r]
                remote(ref, ref, send.at[step, 6], recv_c.at[step, place, part], other_core)

        def issue(k):
            for direction in (4, 5, 0, 1, 2, 3):
                queue = QUEUES[step][direction]
                if k >= len(queue):
                    continue
                rest = pl.ds(WIDE, H - WIDE)
                if direction < 4:
                    place, chunk = queue[k]
                    ensure_a(place, chunk)
                    early = place == (0, 0) and chunk in (0, 2)
                    send_chunk(step, a, direction, place, chunk, rest if early else pl.ds(0, H))
                else:
                    place, part, chunk = queue[k]
                    ensure_b(place, part, chunk)
                    if step == 1:
                        send_piece(step, b1, direction, place, 0, chunk, rest if place == 0 and chunk < 2 else None)
                    elif (direction, place, part, chunk) != (4, 0, 0, 0):
                        send_piece(step, parts[part], direction, place, part, chunk)

        def products(region, count, mine, shared, before):
            count0, mine0, shared0 = before
            order = ORDERS[region]
            items = []
            for i in range(count0, count):
                dx, dy = order[i]
                panel = ((x + dx) % NX) * NY + (y + dy) % NY
                rp = panel % 2
                dz = (panel // 2 + NZ - z) % NZ
                far = jnp.where(dz > 4, NZ - dz, dz)
                reach = jnp.where(rp == r, mine, shared)
                items.append((jnp.int32(slot_of((dx, dy))), dz, rp, jnp.where(far <= reach, 1, 0)))
            for reach0, reach, other in ((mine0, mine, 0), (shared0, shared, 1)):
                for near in range(reach0 + 1, reach + 1):
                    for dz in sorted({near, (NZ - near) % NZ}):
                        place, ranks = meets[dz * 2 + other]
                        rp = 1 - r if other else r
                        items.append((place, jnp.int32(dz), rp, jnp.where(ranks[region] < count0, 1, 0)))

            if not items:
                return
            total, picks = jnp.int32(0), []
            for slot, dz, rp, ready in items:
                picks.append((jnp.where(ready > 0, total, -1), slot * 16 + dz * 2 + rp))
                total = total + ready

            def add(first, size):
                slots, halves = [], []
                for n in range(size):
                    code = jnp.int32(0)
                    for rank, item in picks:
                        code = jnp.where(rank == first + n, item, code)
                    slots.append(lax.div(code, 16))
                    halves.append((lax.rem(lax.div(code, 2), NZ), lax.rem(code, 2)))
                if region == 0:
                    terms = [(upper, COLS[0], wide0)]
                elif region == 1:
                    terms = [(lower, COLS[0], wide0), (full, COLS[1], slim0)]
                else:
                    terms = [(full, full, b1)]
                for rows, cols, b in terms:
                    left = jnp.concatenate([a[slot, rows] for slot in slots], axis=1)
                    right = jnp.concatenate([b[dz, rp] for dz, rp in halves], axis=0)
                    acc[rows, cols] += jnp.dot(left, right, preferred_element_type=jnp.float32)

            size = GROUP
            while size > len(items):
                size //= 2

            @pl.loop(0, total // size)
            def _(j):
                add(j * size, size)

            while size > 1:
                size //= 2

                @pl.when(total // size % 2 == 1)
                def _():
                    add(total // (2 * size) * (2 * size), size)

        issue(0)
        issue(1)
        for part in range(len(parts)):
            share(0, part)
        issue(2)
        acc[...] = jnp.zeros_like(acc)

        before = [(0, -1, -1)] * 3
        stages = list(STAGES[step])
        for k in range(3, 15):
            issue(k)
            while stages and stages[0][0] == k + 1:
                _, region, count, mine, shared = stages.pop(0)
                needed = range(1 if region == 0 else len(parts))
                for place in ORDERS[region][:count]:
                    for chunk in (0, 2) if region == 0 else (0, 1, 2, 3):
                        ensure_a(place, chunk)
                for near in range(0, mine + 1):
                    for dz in sorted({near, (NZ - near) % NZ}):
                        for part in needed:
                            for chunk in range(H // Z_ROWS[step]):
                                ensure_b(dz, part, chunk)
                for near in range(0, shared + 1):
                    for dz in sorted({near, (NZ - near) % NZ}):
                        for part in needed:
                            ensure_c(dz, part)
                if not stages:
                    for direction, queue in enumerate(QUEUES[step]):
                        arrived(a.at[pl.ds(0, len(queue)), pl.ds(0, CH)], send.at[step, direction])
                    arrived(a.at[pl.ds(0, NZ)], send.at[step, 6])
                products(region, count, mine, shared, before[region])
                before[region] = (count, mine, shared)
                if step == 0 and region == 0 and (count, mine, shared) == (16, 4, 4):
                    masked = lambda rows, cols: masked_store(
                        lambda i, j: keep[0, i, j], lambda i, j: acc[i, j], store_second, rows, cols
                    )
                    load_keep.wait()
                    masked(upper, COLS[0])
                    send_early(1, a1)

        if step == 0:
            masked(upper, COLS[1])
            masked(lower, full)

    copies = []
    for i in range(3):
        rows = slice(i * BS, (i + 1) * BS)
        there = pl.ds(pl.multiple_of(r * H + i * BS, BS), BS)
        for j in range(3):
            cols = slice(j * BS, (j + 1) * BS)
            block = 2.0 * a1[0, rows, cols].astype(jnp.float32) - acc[rows, cols]
            kept = keep[1, z * 6 + r * 3 + i, col * 3 + j] > 0
            out[there, cols] = jnp.where(kept, block, jnp.zeros_like(block)).astype(jnp.bfloat16)
        copy = pltpu.make_async_remote_copy(
            src_ref=out.at[there], dst_ref=out.at[there], send_sem=misc.at[3 + i], recv_sem=misc.at[6 + i],
            device_id=other_core, device_id_type=MESH,
        )
        copy.start()
        copies.append(copy)
    for copy in copies:
        copy.wait()


def shards(density, pattern, keep):
    hbm = pl.BlockSpec(memory_space=pl.ANY)
    bf16 = jnp.bfloat16
    return pl.pallas_call(
        kernel,
        out_shape=pltpu.VMEM(density.shape, bf16),
        in_specs=[hbm, hbm, hbm],
        out_specs=pl.BlockSpec(memory_space=pltpu.VMEM),
        scratch_shapes=[
            pltpu.VMEM((NX * NY, H, H), bf16),
            pltpu.VMEM((NX * NY, H, H), bf16),
            pltpu.VMEM((NZ, 2, H, WIDE), bf16),
            pltpu.VMEM((NZ, 2, H, H - WIDE), bf16),
            pltpu.VMEM((NZ, 2, H, H), bf16),
            pltpu.VMEM((H, H), jnp.float32),
            pltpu.VMEM((H, H), bf16),
            pltpu.SMEM(pattern.shape, jnp.int32),
            pltpu.SMEM(keep.shape, jnp.int32),
            pltpu.SemaphoreType.DMA((2, NX * NY, 4)),
            pltpu.SemaphoreType.DMA((2, NZ, 2, 4)),
            pltpu.SemaphoreType.DMA((2, NZ, 2)),
            pltpu.SemaphoreType.DMA((2, 7)),
            pltpu.SemaphoreType.DMA((9,)),
        ],
        name="purify",
        cost_estimate=pl.CostEstimate(flops=2 * 2 * H * H * 6144, bytes_accessed=2 * 768 * H * 2, transcendentals=0),
        compiler_params=pltpu.CompilerParams(
            collective_id=0, has_side_effects=True, vmem_limit_bytes=60 * 2**20
        ),
    )(pattern, keep, density)


def solution(mesh):
    in_specs = (P("row", "col"), P(), P())
    out_specs = P("row", "col")
    return jax.shard_map(shards, mesh=mesh, in_specs=in_specs, out_specs=out_specs, check_vma=False)
```
